1024 devices in a mesh: prow: 16 (over z_hi, y), pcol: 64 (over x, z_lo, core).
Axes of the slice: x: 4, y: 4, z: 32 (z_hi: 4, z_lo: 8; z = z_hi * 8 + z_lo), core: 2. Of those that a mesh axis runs over, the one named last changes fastest.
Arguments:
- matrix: float32 [8192, 8192], P('prow', 'pcol'), may hold values from -6 to 6
- panel: float32 [8192, 1024], P(('prow', 'pcol')), as said below
- pivots: int32 [1024], replicated, may hold values from 0 to 8191, as said below
Outputs:
- trailing: float32 [8192, 8192], P('prow', 'pcol')
The draws below stay inside these ranges and needn't reach their ends.
Inputs may be any that keep to these rules, and one draw needn't show every extreme that they name: pivots[i] is either i itself or a row at or beyond 1024; the rows at or beyond 1024 that are named are all different; at most 44 of them lie in the rows of one index of prow, and some index of prow holds exactly 44. `panel`: the top 1024 rows are unit lower triangular.
All inputs are finite; a program needn't handle non-finite values.
Results may differ from the reference program's by a relative error of at most 0.000061.
Values sent between devices are 32-bit elements; how exact they have to be, the bound alone decides.
A program may use at most 32 MiB of HBM per device.

```python
import jax
import jax.numpy as jnp
from jax import lax

NB = 1024
ROWS_DEV = 512
NROWS = 8192
NCOLS = 8192
CAP = 44


def draw_pivots(key, part):
    sources = NB // ROWS_DEV
    count = NROWS // ROWS_DEV - sources
    moved_total = NB // 2
    local = jax.vmap(lambda sub: jax.random.permutation(sub, ROWS_DEV))(jax.random.split(jax.random.fold_in(key, 31), count))
    last_perm = local[count - 1]
    where_last = jnp.argmax(last_perm == ROWS_DEV - 1)
    swapped = last_perm.at[where_last].set(last_perm[0]).at[0].set(ROWS_DEV - 1)
    local = local.at[count - 1].set(swapped)
    candidates = (jnp.arange(count)[:, None] + sources) * ROWS_DEV + local[:, :CAP]
    planted = jax.random.randint(jax.random.fold_in(key, 32), (), 0, count)
    order_score = jax.random.permutation(jax.random.fold_in(key, 33), count)
    devices = jnp.arange(count)
    score = jnp.where(devices == planted, -2, jnp.where(devices == count - 1, -1, order_score))
    device_order = jnp.argsort(score)
    flat = candidates[device_order].reshape(-1)
    ranking = jax.random.permutation(jax.random.fold_in(key, 34), NB)
    targets = flat[jnp.minimum(ranking, count * CAP - 1)]
    return jnp.where(ranking < moved_total, targets, jnp.arange(NB)).astype(jnp.int32)


def draw_panel(key, part):
    base = jax.random.normal(jax.random.fold_in(key, 21), (NROWS, NB), jnp.float32)
    base = base / NB ** 0.5
    row_ids = jnp.arange(NROWS)[:, None]
    col_ids = jnp.arange(NB)[None, :]
    lower_tri = jnp.where(col_ids < row_ids, base, 0.0) + jnp.where(col_ids == row_ids, 1.0, 0.0)
    return jnp.where(row_ids < NB, lower_tri, base).astype(jnp.float32)


def shard_levels(own_key, dims, shards, low, top_value):
    factor_of = 1.0
    for position, shards_of in shards:
        steps = jax.random.uniform(jax.random.fold_in(jax.random.fold_in(own_key, 6), position), (shards_of,), jnp.float32, low / len(shards), top_value / len(shards))
        factor_of = factor_of * jnp.repeat(jnp.exp(steps), dims[position] // shards_of).reshape((-1,) + (1,) * (len(dims) - 1 - position))
    return factor_of


def centred(rng, shape, width, bound, shards=(), held_as=jnp.bfloat16):
    values = width * jax.random.normal(rng, shape, jnp.float32)
    if shards:
        values = values * shard_levels(rng, shape, shards, -0.22, 0.18)
    return jnp.clip(values, -bound, bound).astype(held_as)


def setup_inputs(seed: int = 0) -> dict:
    key_of = jax.random.split(jax.random.key(seed), 4)
    matrix = centred(key_of[0], (NROWS, NCOLS), 1.0, 6.0, ((0, 16), (1, 64)), jnp.float32)
    panel = draw_panel(jax.random.fold_in(key_of[3], 71), 0)
    pivots = draw_pivots(jax.random.fold_in(key_of[3], 71), 0)
    return {"matrix": matrix, "panel": panel, "pivots": pivots}


def reference(matrix, panel, pivots):
    total = matrix.shape[0]
    block = pivots.shape[0]
    order = jnp.arange(total, dtype=jnp.int32)
    order = order.at[:block].set(pivots.astype(jnp.int32))
    target = jnp.where(pivots >= block, pivots, total).astype(jnp.int32)
    order = order.at[target].set(jnp.arange(block, dtype=jnp.int32), mode="drop")
    permuted = jnp.take(matrix, order, axis=0)
    upper = jnp.dot(panel[:block], permuted[:block], precision=lax.Precision.HIGHEST, preferred_element_type=jnp.float32)
    lower = permuted[block:] - jnp.dot(panel[block:], upper, precision=lax.Precision.HIGHEST, preferred_element_type=jnp.float32)
    return jnp.concatenate([upper, lower], axis=0)
```

```python
import jax
import jax.numpy as jnp
from jax import lax
from jax.experimental import pallas as pl
from jax.experimental.pallas import tpu as pltpu
from jax.sharding import PartitionSpec as P

MESH = pl.DeviceIdType.MESH
F32, BF16, I32 = jnp.float32, jnp.bfloat16, jnp.int32

ZH, Y, X, ZL, C = 4, 4, 4, 8, 2
ROWS, NB, COLS = 512, 1024, 128
BLK = ROWS // (X * ZL * C)
KC = 48
HK = KC // 2
SLOTS = ZH * Y * KC
CH, NCH = 64, 4
TILE = ROWS // X
NATURAL = (0, 3, 1, 2)
BITS = ZL.bit_length() - 1


def rev(s):
    return sum(((s >> j) & 1) << (BITS - 1 - j) for j in range(BITS))


def dot(a, b):
    return jnp.dot(a, b, preferred_element_type=F32)


def split(a):
    hi = a.astype(BF16)
    return hi, (a - hi.astype(F32)).astype(BF16)


def split3(a):
    hi = a.astype(BF16)
    rest = a - hi.astype(F32)
    mid = rest.astype(BF16)
    return hi, mid, (rest - mid.astype(F32)).astype(BF16)


def kernel(
    mat, pan_in, piv, out,
    pan, phi, plo, vloc, vfwd, vall, vhl, tt, thm, tlo, slots, slotc, phl,
    dall, dme, dfwd, base, ub, uhl, send, recv,
):
    prow, pcol = lax.axis_index("prow"), lax.axis_index("pcol")
    zh, y = prow // Y, prow % Y
    x, zl, c = pcol // (ZL * C), (pcol // C) % ZL, pcol % C

    def at(zh=zh, y=y, x=x, zl=zl, c=c):
        return (zh * Y + y, x * (ZL * C) + zl * C + c)

    def bit(j):
        return (zl // (1 << j)) % 2

    ydev = [at(y=(y + d) % Y) for d in range(Y)]
    xdev = [at(x=(x + d) % X) for d in range(X)]
    zdev = [at(zl=zl + (1 << j) - (2 << j) * bit(j)) for j in range(BITS)]
    other = at(c=1 - c)
    up, down = at(zh=(zh + 1) % ZH), at(zh=(zh + ZH - 1) % ZH)
    partners = ydev[1:] + xdev[1:] + zdev + [other, up, down]

    names = {}

    def num(key):
        return names.setdefault(key, len(names))

    counter = [0]

    def rc(src, dst, key, dev):
        sid = counter[0]
        counter[0] += 1
        return pltpu.make_async_remote_copy(
            src_ref=src, dst_ref=dst, send_sem=send.at[sid], recv_sem=recv.at[num(key)],
            device_id=dev, device_id_type=MESH,
        )

    def arrived(dst, key):
        pltpu.make_async_remote_copy(
            src_ref=dst, dst_ref=dst, send_sem=send.at[0], recv_sem=recv.at[num(key)],
            device_id=other, device_id_type=MESH,
        ).wait_recv()

    pending = []

    def start(copies, cond=None):
        pending.append((cond, copies))
        if cond is None:
            for cp in copies:
                cp.start()
        else:
            @pl.when(cond)
            def _():
                for cp in copies:
                    cp.start()

    barrier = pltpu.get_barrier_semaphore()
    for dev in partners:
        pl.semaphore_signal(barrier, inc=1, device_id=dev, device_id_type=MESH)

    prowv = piv[...]
    named = prowv >= NB
    group = (prowv // ROWS) % Y * ZH + (prowv // ROWS) // Y
    onehot = jnp.where(
        (lax.broadcasted_iota(I32, (ZH * Y, NB), 0) == group) & named, 1.0, 0.0
    ).astype(F32)
    tri = jnp.where(
        lax.broadcasted_iota(I32, (128, 128), 0) < lax.broadcasted_iota(I32, (128, 128), 1), 1.0, 0.0
    ).astype(BF16)
    before = jnp.zeros((ZH * Y, 1), F32)
    ranks = []
    for b in range(NB // 128):
        part = onehot[:, b * 128:(b + 1) * 128]
        count = dot(part.astype(BF16), tri) + before
        ranks.append(jnp.sum(count * part, axis=0, keepdims=True))
        before = before + jnp.sum(part, axis=1, keepdims=True)
    rank = jnp.concatenate(ranks, axis=1)
    slot = jnp.where(named, group.astype(F32) * KC + rank, -1.0)
    slots[...] = jnp.broadcast_to(slot, (8, NB))

    me = (y * ZH + zh) * KC
    kk = lax.broadcasted_iota(I32, (128, NB), 0)
    mine = (kk < KC) & ((kk + me).astype(F32) == slot)
    where_row = jnp.sum(
        jnp.where(mine, (prowv - prow * ROWS + 1).astype(F32), 0.0), axis=1, keepdims=True
    ) - 1.0
    pick = jnp.where(
        lax.broadcasted_iota(I32, (128, ROWS), 1).astype(F32) == where_row, 1.0, 0.0
    ).astype(F32)
    mh, mm, ml = split3(mat[...])
    pick16 = pick[:KC].astype(BF16)
    vloc[...] = (dot(pick16, mh) + dot(pick16, mm)) + dot(pick16, ml)
    dme[KC:, :] = jnp.zeros((128 - KC, COLS), F32)

    top = zh == 0
    root = top & (y < 2)
    inner = (zh == 1) | (zh == 3)

    @pl.when(top)
    def _():
        vall[y, 0] = vloc[...]

    @pl.when(root)
    def _():
        tt[y] = mat[...]

    pl.semaphore_wait(barrier, len(partners))

    s_own = sum(bit(j) * (1 << (BITS - 1 - j)) for j in range(BITS))
    j0 = BITS - 1
    pan[x, c, s_own] = pan_in[...]
    start([rc(pan_in, pan.at[x, c, s_own], "pz0", zdev[j0])])
    start([rc(vloc, vall.at[y, 1], "v1", down)], zh == 1)
    start([rc(vloc, vall.at[y, 3], "v3", up)], zh == 3)
    start([rc(vloc.at[pl.ds(0, HK)], vfwd, "vf", down),
           rc(vloc.at[pl.ds(HK, HK)], vfwd, "vf", up)], zh == 2)
    start([rc(mat, tt.at[0], "t0", ydev[1])], top & (y == 0))

    def to_roots(z):
        for d in range(1, Y):
            target = (y + d) % Y
            start([rc(vall.at[y, z], vall.at[y, z], ("vy", d, z), ydev[d])], top & (target < 2))

    to_roots(0)

    for t in range(BITS):
        j = BITS - 1 - t
        size = 1 << t
        base_in = (s_own // size) * size
        theirs = base_in + (size - 2 * size * ((s_own // size) % 2))
        arrived(pan.at[x, c, pl.ds(theirs, size)] if t else pan.at[x, c, theirs], ("pz%d" % t))
        if t + 1 < BITS:
            nxt = 2 * size
            have = (s_own // nxt) * nxt
            start([rc(pan.at[x, c, pl.ds(have, nxt)], pan.at[x, c, pl.ds(have, nxt)],
                      "pz%d" % (t + 1), zdev[j - 1])])
        if t == 1:
            @pl.when(inner)
            def _():
                arrived(vfwd, "vf")
            start([rc(vfwd, vall.at[y, 2, pl.ds(0, HK)], "v2a", down)], zh == 1)
            start([rc(vfwd, vall.at[y, 2, pl.ds(HK, HK)], "v2b", up)], zh == 3)

    for d in (2, 1, 3):
        start([rc(pan.at[x, c], pan.at[x, c], ("px", d), xdev[d])])
    start([rc(pan.at[x, c], pan.at[x, c], ("pc", 0), other)])

    @pl.when(top)
    def _():
        arrived(vall.at[y, 1], "v1")
    to_roots(1)

    @pl.when(top)
    def _():
        arrived(vall.at[y, 3], "v3")
    to_roots(3)

    @pl.when(root & (y == 1))
    def _():
        arrived(tt.at[0], "t0")

    @pl.when(root)
    def _():
        def tops(i, carry):
            for h in range(2):
                hi, mid, lo = split3(tt[h, pl.ds(i * 128, 128), :])
                at_row = pl.ds(h * ROWS + i * 128, 128)
                thm[at_row, 0:128] = hi
                thm[at_row, 128:256] = mid
                tlo[at_row, :] = lo
            return carry

        @pl.when(y == 0)
        def _():
            tt[1] = jnp.zeros((ROWS, COLS), F32)
        lax.fori_loop(0, ROWS // 128, tops, 0)

    @pl.when(root & (y == 1))
    def _():
        def pack(i, carry):
            ss = lax.broadcasted_iota(I32, (ZH * KC, NB), 0) + i * (ZH * KC)
            got = jnp.where(ss.astype(F32) == slots[0:1, :], 1.0, 0.0).astype(BF16)
            two = dot(got, thm[...])
            all3 = (two[:, :128] + two[:, 128:]) + dot(got, tlo[...])
            for z in range(ZH):
                dall[i, z] = all3[z * KC:(z + 1) * KC]
            return carry
        lax.fori_loop(0, Y, pack, 0)

    for d in range(1, Y):
        start([rc(dall.at[(y + d) % Y], dall.at[(y + d) % Y], "dy", ydev[d])], top & (y == 1))

    @pl.when(top)
    def _():
        arrived(vall.at[y, 2, pl.ds(0, HK)], "v2a")
        arrived(vall.at[y, 2, pl.ds(HK, HK)], "v2b")
    to_roots(2)

    @pl.when(top & (y != 1))
    def _():
        arrived(dall.at[y], "dy")
    start([rc(dall.at[y, 1], dme.at[pl.ds(0, KC)], "d", up),
           rc(dall.at[y, 3], dme.at[pl.ds(0, KC)], "d", down),
           rc(dall.at[y, 2, pl.ds(0, HK)], dfwd, "df", up),
           rc(dall.at[y, 2, pl.ds(HK, HK)], dfwd, "df", down)], top)

    @pl.when(root)
    def _():
        slotc[...] = jnp.transpose(jnp.broadcast_to(slots[0:1, :], (128, NB)))
        for d in range(1, Y):
            src = (y + Y - d) % Y
            for z in range(ZH):
                arrived(vall.at[src, z], ("vy", d, z))

        def vsplit(i, carry):
            for z in range(ZH):
                hi, lo = split(vall[i, z])
                vhl[pl.ds(i * (ZH * KC) + z * KC, KC), 0:128] = hi
                vhl[pl.ds(i * (ZH * KC) + z * KC, KC), 128:256] = lo
            return carry
        lax.fori_loop(0, Y, vsplit, 0)

        def form(i, carry):
            rows = pl.ds(i * 128, 128)
            sc = slotc[rows, :]
            lane = lax.broadcasted_iota(I32, (128, 128), 1)
            sel = jnp.concatenate(
                [jnp.where((lane + b * 128).astype(F32) == sc, 1.0, 0.0).astype(BF16)
                 for b in range(SLOTS // 128)], axis=1)
            moved = dot(sel, vhl[...])
            stay = jnp.concatenate([sc, sc], axis=1) < 0.0
            phl[rows, :] = jnp.where(stay, thm[rows, :].astype(F32), moved).astype(BF16)
            return carry

        @pl.when(y == 0)
        def _():
            phl[ROWS:, :] = jnp.zeros((ROWS, 2 * COLS), BF16)
        lax.fori_loop(0, 4 + 4 * y, form, 0)

    for d in (1, 3, 2):
        src = (x + X - d) % X
        arrived(pan.at[src, c], ("px", d))
        start([rc(pan.at[src, c], pan.at[src, c], ("pc", d), other)])
    for d in (0, 1, 3, 2):
        arrived(pan.at[(x + X - d) % X, 1 - c], ("pc", d))

    def psplit(i, carry):
        for cc in range(C):
            for s in range(ZL):
                hi, lo = split(pan[i, cc, s])
                rows = pl.ds((cc * ZL + s) * BLK, BLK)
                phi[i, rows, :] = hi
                plo[i, rows, :] = lo
        return carry
    lax.fori_loop(0, X, psplit, 0)

    def blocks(i, right, store):
        two = dot(phi[i], right[...])
        res = (two[:, :128] + two[:, 128:]) + dot(plo[i], right[:, 0:128])
        for cc in range(C):
            for s in range(ZL):
                k = cc * ZL + s
                store(i * TILE + BLK * (rev(s) * C + cc), res[k * BLK:(k + 1) * BLK])

    def u_half(h):
        line = y + h * (3 - 2 * y)

        @pl.when(root)
        def _():
            def store(row, val):
                ub[line, pl.ds(row - h * (ROWS // 2), BLK), :] = val
                out[pl.ds(row, BLK), :] = val

            def tile(i, carry):
                blocks(i, phl, store)
                return carry
            lax.fori_loop(2 * h, 2 * h + 2, tile, 0)

    def chunk(line, k):
        return ub.at[line, pl.ds(k * CH, CH)]

    def send_u(line, k, dev, cond):
        start([rc(chunk(line, k), chunk(line, k), ("u", k, "line"), dev)], cond)

    def ukey(rel, k):
        return ("u", rel, k)

    def send_chunk(line, rel, k, dev, cond):
        start([rc(chunk(line, k), chunk(line, k), ukey(rel, k), dev)], cond)

    r0, r1 = top & (y == 0), top & (y == 1)
    u_half(1)
    for k in range(NCH):
        send_chunk(3, 0, k, ydev[3], r0)
        send_chunk(2, 0, k, ydev[1], r1)
    u_half(0)
    order_up, order_down = (0, 1, 2, 3), (2, 3, 0, 1)
    for a, b in zip(order_up, order_down):
        send_chunk(y, 0, a, up, root)
        send_chunk(y, 0, b, down, root)
    for k in range(NCH):
        send_chunk(3, 1, k, ydev[2], r0)
        send_chunk(0, 2, k, ydev[2], r0)
        send_chunk(0, 1, k, ydev[3], r0)
        send_chunk(1, 3, k, ydev[1], r1)
        send_chunk(1, 2, k, ydev[2], r1)
        send_chunk(2, 3, k, ydev[2], r1)

    nonroot = top & (y >= 2)
    for a, b in zip(order_up, order_down):
        @pl.when(nonroot)
        def _():
            if a < 2:
                arrived(chunk(y, a), ukey(0, a))
                arrived(chunk(y, b), ukey(0, b))
        send_chunk(y, 0, a, up, nonroot)
        send_chunk(y, 0, b, down, nonroot)

    @pl.when(inner)
    def _():
        arrived(dfwd, "df")
    start([rc(dfwd, dme.at[pl.ds(0, HK)], "d2a", up)], zh == 1)
    start([rc(dfwd, dme.at[pl.ds(HK, HK)], "d2b", down)], zh == 3)

    @pl.when(nonroot)
    def _():
        dme[0:KC, :] = dall[y, 0]

    @pl.when(inner)
    def _():
        arrived(dme.at[pl.ds(0, KC)], "d")

    @pl.when(zh == 2)
    def _():
        arrived(dme.at[pl.ds(0, HK)], "d2a")
        arrived(dme.at[pl.ds(HK, HK)], "d2b")

    notroot = (zh > 0) | (y >= 2)

    @pl.when(notroot)
    def _():
        scat = jnp.transpose(pick)
        hit = jnp.sum(scat, axis=1, keepdims=True) > 0.0
        dh, dm, dl = split3(dme[...])
        scat16 = scat.astype(BF16)
        moved = (dot(scat16, dh) + dot(scat16, dm)) + dot(scat16, dl)
        base[...] = jnp.where(hit, moved, mat[...])

    for z, order in ((1, order_up), (3, order_down), (2, (0, 2, 1, 3))):
        for k in order:
            @pl.when(zh == z)
            def _():
                arrived(chunk(y, k), ukey(0, k))
            if z == 1 and k < 2:
                send_chunk(y, 0, k, up, zh == 1)
            if z == 3 and k >= 2:
                send_chunk(y, 0, k, down, zh == 3)
            for d in (2, 1, 3):
                send_chunk(y, Y - d, k, ydev[d], zh == z)

    @pl.when(notroot)
    def _():
        for rel in range(1, Y):
            for k in range(NCH):
                arrived(chunk((y + rel) % Y, k), ukey(rel, k))

        for q, line in enumerate(NATURAL):
            hi, lo = split(ub[line])
            uhl[q * 256:(q + 1) * 256, 0:128] = hi
            uhl[q * 256:(q + 1) * 256, 128:256] = lo

        def store(row, val):
            out[pl.ds(row, BLK), :] = base[pl.ds(row, BLK), :] - val

        def tile(i, carry):
            blocks(i, uhl, store)
            return carry
        lax.fori_loop(0, X, tile, 0)

    for cond, copies in pending:
        if cond is None:
            for cp in copies:
                cp.wait_send()
        else:
            @pl.when(cond)
            def _(copies=copies):
                for cp in copies:
                    cp.wait_send()


def per_device(matrix, panel, pivots):
    vmem = pl.BlockSpec(memory_space=pltpu.VMEM)
    return pl.pallas_call(
        kernel,
        out_shape=jax.ShapeDtypeStruct((ROWS, COLS), F32),
        in_specs=[vmem] * 3,
        out_specs=vmem,
        scratch_shapes=[
            pltpu.VMEM((X, C, ZL, BLK, NB), F32),
            pltpu.VMEM((X, TILE, NB), BF16),
            pltpu.VMEM((X, TILE, NB), BF16),
            pltpu.VMEM((KC, COLS), F32),
            pltpu.VMEM((HK, COLS), F32),
            pltpu.VMEM((Y, ZH, KC, COLS), F32),
            pltpu.VMEM((SLOTS, 2 * COLS), BF16),
            pltpu.VMEM((2, ROWS, COLS), F32),
            pltpu.VMEM((NB, 2 * COLS), BF16),
            pltpu.VMEM((NB, COLS), BF16),
            pltpu.VMEM((8, NB), F32),
            pltpu.VMEM((NB, 128), F32),
            pltpu.VMEM((NB, 2 * COLS), BF16),
            pltpu.VMEM((Y, ZH, KC, COLS), F32),
            pltpu.VMEM((128, COLS), F32),
            pltpu.VMEM((HK, COLS), F32),
            pltpu.VMEM((ROWS, COLS), F32),
            pltpu.VMEM((4, ROWS // 2, COLS), F32),
            pltpu.VMEM((NB, 2 * COLS), BF16),
            pltpu.SemaphoreType.DMA((192,)),
            pltpu.SemaphoreType.DMA((64,)),
        ],
        compiler_params=pltpu.CompilerParams(
            collective_id=0, has_side_effects=True, vmem_limit_bytes=40 * 2**20
        ),
    )(matrix, panel, pivots.reshape(1, NB))


def solution(mesh):
    placed = (P("prow", "pcol"), P(("prow", "pcol"), None), P())
    return jax.shard_map(
        per_device, mesh=mesh, in_specs=placed, out_specs=P("prow", "pcol"), check_vma=False
    )
```

```python
import jax
import jax.numpy as jnp
from jax import lax
from jax.experimental import pallas as pl
from jax.experimental.pallas import tpu as pltpu
from jax.sharding import PartitionSpec as P

MESH = pl.DeviceIdType.MESH
F32, BF16, I32 = jnp.float32, jnp.bfloat16, jnp.int32

ZH, Y, X, ZL, C = 4, 4, 4, 8, 2
ROWS, NB, COLS = 512, 1024, 128
BLK = ROWS // (X * ZL * C)
KC = 48
SLOTS = ZH * Y * KC
CH, NCH = 64, 4
TILE = ROWS // X
NATURAL = (0, 3, 1, 2)
BITS = ZL.bit_length() - 1
HALF = ZL // 2
QR = NB // 4


def rev(s):
    return sum(((s >> j) & 1) << (BITS - 1 - j) for j in range(BITS))


def dot(a, b):
    return jnp.dot(a, b, preferred_element_type=F32)


def split(a):
    hi = a.astype(BF16)
    return hi, (a - hi.astype(F32)).astype(BF16)


def split3(a):
    hi = a.astype(BF16)
    rest = a - hi.astype(F32)
    mid = rest.astype(BF16)
    return hi, mid, (rest - mid.astype(F32)).astype(BF16)


def kernel(
    mat_hbm, pan_hbm, piv_hbm, out,
    mat, piv, pan, phi, plo, vloc, vall, vhl, tt, thm, tlo, slots, slotc, phl,
    dall, dme, dfwd, scat, base, ub, uhl, send, recv, local,
):
    prow, pcol = lax.axis_index("prow"), lax.axis_index("pcol")
    zh, y = prow // Y, prow % Y
    x, zl, c = pcol // (ZL * C), (pcol // C) % ZL, pcol % C

    def at(zh=zh, y=y, x=x, zl=zl, c=c):
        return (zh * Y + y, x * (ZL * C) + zl * C + c)

    def bit(j):
        return (zl // (1 << j)) % 2

    ydev = [at(y=(y + d) % Y) for d in range(Y)]
    xdev = [at(x=(x + d) % X) for d in range(X)]
    zdev = [at(zl=zl + (1 << j) - (2 << j) * bit(j)) for j in range(BITS)]
    other = at(c=1 - c)
    up, down = at(zh=(zh + 1) % ZH), at(zh=(zh + ZH - 1) % ZH)
    near = ydev[1:] + xdev[1:] + zdev + [other]

    names = {}

    def num(key):
        return names.setdefault(key, len(names))

    counter = [0]

    def rc(src, dst, key, dev):
        sid = counter[0]
        counter[0] += 1
        return pltpu.make_async_remote_copy(
            src_ref=src, dst_ref=dst, send_sem=send.at[sid], recv_sem=recv.at[num(key)],
            device_id=dev, device_id_type=MESH,
        )

    def arrived(dst, key):
        pltpu.make_async_remote_copy(
            src_ref=dst, dst_ref=dst, send_sem=send.at[0], recv_sem=recv.at[num(key)],
            device_id=other, device_id_type=MESH,
        ).wait_recv()

    pending = []

    def start(copies, cond=None):
        pending.append((cond, copies))
        if cond is None:
            for cp in copies:
                cp.start()
        else:
            @pl.when(cond)
            def _():
                for cp in copies:
                    cp.start()

    top = zh == 0
    root = top & (y < 2)
    notroot = (zh > 0) | (y >= 2)
    inner = (zh == 1) | (zh == 3)
    early = zl < ZL // 2

    barrier = pltpu.get_barrier_semaphore()

    @pl.when(top)
    def _():
        for z in (2, 1, 3):
            pl.semaphore_signal(barrier, inc=1, device_id=at(zh=z), device_id_type=MESH)
    for dev in near:
        pl.semaphore_signal(barrier, inc=1, device_id=dev, device_id_type=MESH)

    s_own = sum(bit(j) * (1 << (BITS - 1 - j)) for j in range(BITS))
    own = pan.at[x, c, s_own]
    loads = [pltpu.make_async_copy(piv_hbm, piv, local.at[0]),
             pltpu.make_async_copy(mat_hbm, mat, local.at[1]),
             pltpu.make_async_copy(pan_hbm, own, local.at[2])]
    for cp in loads:
        cp.start()
    loads[0].wait()

    def pack_own(prowv, slot):
        me = (y * ZH + zh) * KC
        kk = lax.broadcasted_iota(I32, (128, NB), 0)
        mine = (kk < KC) & ((kk + me).astype(F32) == slot)
        where_row = jnp.sum(
            jnp.where(mine, (prowv - prow * ROWS + 1).astype(F32), 0.0), axis=1, keepdims=True
        ) - 1.0
        pick = jnp.where(
            lax.broadcasted_iota(I32, (128, ROWS), 1).astype(F32) == where_row, 1.0, 0.0
        ).astype(F32)
        mh, mm, ml = split3(mat[...])
        pick16 = pick[:KC].astype(BF16)
        vloc[...] = (dot(pick16, mh) + dot(pick16, mm)) + dot(pick16, ml)
        scat[...] = jnp.transpose(pick).astype(BF16)

    prowv = piv[...]
    named = prowv >= NB
    group = (prowv // ROWS) % Y * ZH + (prowv // ROWS) // Y
    onehot = jnp.where(
        (lax.broadcasted_iota(I32, (ZH * Y, NB), 0) == group) & named, 1.0, 0.0
    ).astype(F32)
    tri = jnp.where(
        lax.broadcasted_iota(I32, (128, 128), 0) < lax.broadcasted_iota(I32, (128, 128), 1), 1.0, 0.0
    ).astype(BF16)
    before = jnp.zeros((ZH * Y, 1), F32)
    ranks = []
    for b in range(NB // 128):
        part = onehot[:, b * 128:(b + 1) * 128]
        count = dot(part.astype(BF16), tri) + before
        ranks.append(jnp.sum(count * part, axis=0, keepdims=True))
        before = before + jnp.sum(part, axis=1, keepdims=True)
    rank = jnp.concatenate(ranks, axis=1)
    slot = jnp.where(named, group.astype(F32) * KC + rank, -1.0)
    slots[...] = jnp.broadcast_to(slot, (8, NB))

    loads[1].wait()

    @pl.when(root)
    def _():
        vloc[...] = jnp.zeros((KC, COLS), F32)
        tt[y] = mat[...]

    @pl.when(notroot)
    def _():
        pack_own(prowv, slot)
    dme[KC:, :] = jnp.zeros((128 - KC, COLS), F32)

    @pl.when(top)
    def _():
        vall[y, 0] = vloc[...]

    loads[2].wait()
    pl.semaphore_wait(barrier, len(near) + (zh + ZH - 1) // ZH)

    j0 = BITS - 1
    start([rc(own, own, "pz0", zdev[j0])])
    start([rc(vloc, vall.at[y, 1], "v1", down)], zh == 1)
    start([rc(vloc, vall.at[y, 3], "v3", up)], zh == 3)
    start([rc(vloc, vall.at[y, 2], "v2", at(zh=(zh + 2) % ZH))], zh == 2)
    start([rc(mat, tt.at[0], "t0", ydev[1])], top & (y == 0))

    def to_roots(z):
        for d in range(1, Y):
            target = (y + d) % Y
            start([rc(vall.at[y, z], vall.at[y, z], ("vy", d, z), ydev[d])], top & (target < 2))

    to_roots(0)

    def to_core(d, piece, first):
        blocks = pan.at[(x + X - d) % X, c, pl.ds(first, HALF)]
        start([rc(blocks, blocks, ("pc", d, piece), other)])

    def over_x(piece, first):
        blocks = pan.at[x, c, pl.ds(first, HALF)]
        for d in (2, 1, 3):
            start([rc(blocks, blocks, ("px", d, piece), xdev[d])])
        to_core(0, piece, first)

    for t in range(BITS):
        j = BITS - 1 - t
        size = 1 << t
        base_in = (s_own // size) * size
        theirs = base_in + (size - 2 * size * ((s_own // size) % 2))
        arrived(pan.at[x, c, pl.ds(theirs, size)] if t else pan.at[x, c, theirs], ("pz%d" % t))
        if t + 1 < BITS:
            nxt = 2 * size
            have = (s_own // nxt) * nxt
            start([rc(pan.at[x, c, pl.ds(have, nxt)], pan.at[x, c, pl.ds(have, nxt)],
                      "pz%d" % (t + 1), zdev[j - 1])])
        if t + 2 == BITS:
            over_x(0, have)

    over_x(1, theirs)

    @pl.when(root & (y == 1))
    def _():
        arrived(tt.at[0], "t0")

    @pl.when(root)
    def _():
        def tops(i, carry):
            for h in range(2):
                hi, mid, lo = split3(tt[h, pl.ds(i * 128, 128), :])
                at_row = pl.ds(h * ROWS + i * 128, 128)
                thm[at_row, 0:128] = hi
                thm[at_row, 128:256] = mid
                tlo[at_row, :] = lo
            return carry

        @pl.when(y == 0)
        def _():
            tt[1] = jnp.zeros((ROWS, COLS), F32)
        lax.fori_loop(0, ROWS // 128, tops, 0)

    @pl.when(root & (y == 1))
    def _():
        def pack(i, carry):
            ss = lax.broadcasted_iota(I32, (ZH * KC, NB), 0) + i * (ZH * KC)
            got = jnp.where(ss.astype(F32) == slots[0:1, :], 1.0, 0.0).astype(BF16)
            two = dot(got, thm[...])
            all3 = (two[:, :128] + two[:, 128:]) + dot(got, tlo[...])
            for z in range(ZH):
                dall[i, z] = all3[z * KC:(z + 1) * KC]
            return carry
        lax.fori_loop(0, Y, pack, 0)

    for d in range(1, Y):
        start([rc(dall.at[(y + d) % Y], dall.at[(y + d) % Y], "dy", ydev[d])], top & (y == 1))

    for z in (1, 3):
        @pl.when(top)
        def _():
            arrived(vall.at[y, z], "v%d" % z)
        to_roots(z)

    for d in (1, 3, 2):
        src = (x + X - d) % X
        arrived(pan.at[src, c, pl.ds(have, HALF)], ("px", d, 0))
        to_core(d, 0, have)

    @pl.when(top & (y != 1))
    def _():
        arrived(dall.at[y], "dy")
    start([rc(dall.at[y, 1], dme.at[pl.ds(0, KC)], "d", up),
           rc(dall.at[y, 3], dme.at[pl.ds(0, KC)], "d", down)], top)

    for d in (1, 3, 2):
        src = (x + X - d) % X
        arrived(pan.at[src, c, pl.ds(theirs, HALF)], ("px", d, 1))
        to_core(d, 1, theirs)

    @pl.when(top)
    def _():
        arrived(vall.at[y, 2], "v2")
    to_roots(2)
    start([rc(dall.at[y, 2], dfwd, "df", up)], top & early)
    start([rc(dall.at[y, 2], dfwd, "df", down)], top & (zl >= ZL // 2))

    for piece, mine_at in enumerate((have, theirs)):
        for d in range(X):
            arrived(pan.at[(x + X - d) % X, 1 - c, pl.ds(mine_at, HALF)], ("pc", d, piece))

    def psplit(i, carry):
        for cc in range(C):
            for s in range(ZL):
                hi, lo = split(pan[i, cc, s])
                rows = pl.ds((cc * ZL + s) * BLK, BLK)
                for q, line in enumerate(NATURAL):
                    phi[i, rows, line * QR:(line + 1) * QR] = hi[:, q * QR:(q + 1) * QR]
                    plo[i, rows, line * QR:(line + 1) * QR] = lo[:, q * QR:(q + 1) * QR]
        return carry
    lax.fori_loop(0, X, psplit, 0)

    @pl.when(root)
    def _():
        slotc[...] = jnp.transpose(jnp.broadcast_to(slots[0:1, :], (128, NB)))
        for d in range(1, Y):
            src = (y + Y - d) % Y
            for z in range(ZH):
                arrived(vall.at[src, z], ("vy", d, z))

        def vsplit(i, carry):
            for z in range(ZH):
                hi, lo = split(vall[i, z])
                vhl[pl.ds(i * (ZH * KC) + z * KC, KC), 0:128] = hi
                vhl[pl.ds(i * (ZH * KC) + z * KC, KC), 128:256] = lo
            return carry
        lax.fori_loop(0, Y, vsplit, 0)

        def form(i, q, line):
            rows = pl.ds(q * QR + i * 128, 128)
            sc = slotc[rows, :]
            lane = lax.broadcasted_iota(I32, (128, 128), 1)
            sel = jnp.concatenate(
                [jnp.where((lane + b * 128).astype(F32) == sc, 1.0, 0.0).astype(BF16)
                 for b in range(SLOTS // 128)], axis=1)
            moved = dot(sel, vhl[...])
            stay = jnp.concatenate([sc, sc], axis=1) < 0.0
            phl[pl.ds(line * QR + i * 128, 128), :] = jnp.where(
                stay, thm[rows, :].astype(F32), moved).astype(BF16)

        def form_two(q, line):
            def body(i, carry):
                form(i, q, line)
                return carry
            lax.fori_loop(0, 2, body, 0)

        form_two(0, NATURAL[0])
        form_two(1, NATURAL[1])

        @pl.when(y == 0)
        def _():
            for line in NATURAL[2:]:
                phl[line * QR:(line + 1) * QR, :] = jnp.zeros((QR, 2 * COLS), BF16)

        @pl.when(y == 1)
        def _():
            form_two(2, NATURAL[2])
            form_two(3, NATURAL[3])

    def blocks(i, right, store, cols=slice(None)):
        two = dot(phi[i, :, cols], right[...])
        res = (two[:, :128] + two[:, 128:]) + dot(plo[i, :, cols], right[:, 0:128])
        for cc in range(C):
            for s in range(ZL):
                k = cc * ZL + s
                store(i * TILE + BLK * (rev(s) * C + cc), res[k * BLK:(k + 1) * BLK])

    def u_tile(i):
        h = i // 2
        line = y + h * (3 - 2 * y)

        @pl.when(root)
        def _():
            def store(row, val):
                ub[line, pl.ds(row - h * QR, BLK), :] = val
                out[pl.ds(row, BLK), :] = val
            blocks(i, phl, store)

    def chunk(line, k):
        return ub.at[line, pl.ds(k * CH, CH)]

    def ukey(rel, k):
        return ("u", rel, k)

    def send_chunk(line, rel, k, dev, cond):
        start([rc(chunk(line, k), chunk(line, k), ukey(rel, k), dev)], cond)

    r0, r1 = top & (y == 0), top & (y == 1)
    per = TILE // CH
    for i in (2, 3, 0, 1):
        u_tile(i)
        for k in range((i % 2) * per, (i % 2 + 1) * per):
            if i >= 2:
                send_chunk(3, 0, k, ydev[3], r0)
                send_chunk(2, 0, k, ydev[1], r1)
            else:
                send_chunk(y, 0, k, up, root)
                send_chunk(y, 0, k, down, root)
    for k in range(NCH):
        send_chunk(3, 1, k, ydev[2], r0)
        send_chunk(0, 2, k, ydev[2], r0)
        send_chunk(0, 1, k, ydev[3], r0)
        send_chunk(1, 3, k, ydev[1], r1)
        send_chunk(1, 2, k, ydev[2], r1)
        send_chunk(2, 3, k, ydev[2], r1)

    nonroot = top & (y >= 2)
    for k in range(NCH):
        @pl.when(nonroot)
        def _():
            arrived(chunk(y, k), ukey(0, k))
        send_chunk(y, 0, k, up, nonroot)
        send_chunk(y, 0, k, down, nonroot)

    via1, via3 = (zh == 1) & early, (zh == 3) & (zl >= ZL // 2)

    @pl.when(via1 | via3)
    def _():
        arrived(dfwd, "df")
    start([rc(dfwd, dme.at[pl.ds(0, KC)], "d", up)], via1)
    start([rc(dfwd, dme.at[pl.ds(0, KC)], "d", down)], via3)

    @pl.when(nonroot)
    def _():
        dme[0:KC, :] = dall[y, 0]

    @pl.when(zh > 0)
    def _():
        arrived(dme.at[pl.ds(0, KC)], "d")

    @pl.when(notroot)
    def _():
        hit = jnp.sum(scat[...].astype(F32), axis=1, keepdims=True) > 0.0
        dh, dm, dl = split3(dme[...])
        moved = (dot(scat[...], dh) + dot(scat[...], dm)) + dot(scat[...], dl)
        base[...] = jnp.where(hit, moved, mat[...])

    for k in range(NCH):
        @pl.when(zh > 0)
        def _():
            arrived(chunk(y, k), ukey(0, k))
        send_chunk(y, 0, k, up, via1)
        send_chunk(y, 0, k, down, via3)
        for d in (2, 1, 3):
            send_chunk(y, Y - d, k, ydev[d], zh > 0)

    @pl.when(notroot)
    def _():
        def line_step(line, last):
            hi, lo = split(ub[line])
            uhl[:, 0:128] = hi
            uhl[:, 128:256] = lo
            at_col = pl.ds(pl.multiple_of(line * QR, QR), QR)

            def store(row, val):
                rows = pl.ds(row, BLK)
                if last:
                    out[rows, :] = base[rows, :] - val
                else:
                    base[rows, :] = base[rows, :] - val

            def tile(i, carry):
                blocks(i, uhl, store, at_col)
                return carry
            lax.fori_loop(0, X, tile, 0)

        line_step(y, False)
        for rel in (1, 3, 2):
            for k in range(NCH):
                arrived(chunk((y + rel) % Y, k), ukey(rel, k))
            line_step((y + rel) % Y, rel == 2)

    for cond, copies in pending:
        if cond is None:
            for cp in copies:
                cp.wait_send()
        else:
            @pl.when(cond)
            def _(copies=copies):
                for cp in copies:
                    cp.wait_send()


def per_device(matrix, panel, pivots):
    hbm, vmem = pl.BlockSpec(memory_space=pltpu.HBM), pl.BlockSpec(memory_space=pltpu.VMEM)
    return pl.pallas_call(
        kernel,
        out_shape=jax.ShapeDtypeStruct((ROWS, COLS), F32),
        in_specs=[hbm] * 3,
        out_specs=vmem,
        scratch_shapes=[
            pltpu.VMEM((ROWS, COLS), F32),
            pltpu.VMEM((1, NB), I32),
            pltpu.VMEM((X, C, ZL, BLK, NB), F32),
            pltpu.VMEM((X, TILE, NB), BF16),
            pltpu.VMEM((X, TILE, NB), BF16),
            pltpu.VMEM((KC, COLS), F32),
            pltpu.VMEM((Y, ZH, KC, COLS), F32),
            pltpu.VMEM((SLOTS, 2 * COLS), BF16),
            pltpu.VMEM((2, ROWS, COLS), F32),
            pltpu.VMEM((NB, 2 * COLS), BF16),
            pltpu.VMEM((NB, COLS), BF16),
            pltpu.VMEM((8, NB), F32),
            pltpu.VMEM((NB, 128), F32),
            pltpu.VMEM((NB, 2 * COLS), BF16),
            pltpu.VMEM((Y, ZH, KC, COLS), F32),
            pltpu.VMEM((128, COLS), F32),
            pltpu.VMEM((KC, COLS), F32),
            pltpu.VMEM((ROWS, 128), BF16),
            pltpu.VMEM((ROWS, COLS), F32),
            pltpu.VMEM((4, ROWS // 2, COLS), F32),
            pltpu.VMEM((QR, 2 * COLS), BF16),
            pltpu.SemaphoreType.DMA((192,)),
            pltpu.SemaphoreType.DMA((64,)),
            pltpu.SemaphoreType.DMA((3,)),
        ],
        compiler_params=pltpu.CompilerParams(
            collective_id=0, has_side_effects=True, vmem_limit_bytes=40 * 2**20
        ),
    )(matrix, panel, pivots.reshape(1, NB))


def solution(mesh):
    placed = (P("prow", "pcol"), P(("prow", "pcol"), None), P())
    return jax.shard_map(
        per_device, mesh=mesh, in_specs=placed, out_specs=P("prow", "pcol"), check_vma=False
    )
```

```python
import jax
import jax.numpy as jnp
from jax import lax
from jax.experimental import pallas as pl
from jax.experimental.pallas import tpu as pltpu
from jax.sharding import PartitionSpec as P

MESH = pl.DeviceIdType.MESH
F32, BF16, I32 = jnp.float32, jnp.bfloat16, jnp.int32

ZH, Y, X, ZL, C = 4, 4, 4, 8, 2
ROWS, NB, COLS = 512, 1024, 128
BLK = ROWS // (X * ZL * C)
KC = 48
SLOTS = ZH * Y * KC
CH, NCH = 64, 4
TILE = ROWS // X
NATURAL = (0, 3, 1, 2)
BITS = ZL.bit_length() - 1
HALF = ZL // 2
QR = NB // 4
MIDDLE = 4
UPS = 5


def rev(s):
    return sum(((s >> j) & 1) << (BITS - 1 - j) for j in range(BITS))


def dot(a, b):
    return jnp.dot(a, b, preferred_element_type=F32)


def split(a):
    hi = a.astype(BF16)
    return hi, (a - hi.astype(F32)).astype(BF16)


def split3(a):
    hi = a.astype(BF16)
    rest = a - hi.astype(F32)
    mid = rest.astype(BF16)
    return hi, mid, (rest - mid.astype(F32)).astype(BF16)


def kernel(
    mat_hbm, pan_hbm, piv_hbm, out,
    mat, piv, pan, phi, plo, vloc, vall, vhl, tt, thm, tlo, slots, slotc, phl,
    dall, dme, dfwd, scat, sel, base, ub, uhl, send, recv, local, token,
):
    prow, pcol = lax.axis_index("prow"), lax.axis_index("pcol")
    zh, y = prow // Y, prow % Y
    x, zl, c = pcol // (ZL * C), (pcol // C) % ZL, pcol % C

    def at(zh=zh, y=y, x=x, zl=zl, c=c):
        return (zh * Y + y, x * (ZL * C) + zl * C + c)

    def bit(j):
        return (zl // (1 << j)) % 2

    ydev = [at(y=(y + d) % Y) for d in range(Y)]
    xdev = [at(x=(x + d) % X) for d in range(X)]
    zdev = [at(zl=zl + (1 << j) - (2 << j) * bit(j)) for j in range(BITS)]
    other = at(c=1 - c)
    up, down = at(zh=(zh + 1) % ZH), at(zh=(zh + ZH - 1) % ZH)
    near = ydev[1:] + xdev[1:] + zdev + [other]

    names = {}

    def num(key):
        return names.setdefault(key, len(names))

    counter = [0]

    def rc(src, dst, key, dev):
        sid = counter[0]
        counter[0] += 1
        return pltpu.make_async_remote_copy(
            src_ref=src, dst_ref=dst, send_sem=send.at[sid], recv_sem=recv.at[num(key)],
            device_id=dev, device_id_type=MESH,
        )

    def arrived(dst, key):
        pltpu.make_async_remote_copy(
            src_ref=dst, dst_ref=dst, send_sem=send.at[0], recv_sem=recv.at[num(key)],
            device_id=other, device_id_type=MESH,
        ).wait_recv()

    pending = []

    def start(copies, cond=None):
        pending.append((cond, copies))
        if cond is None:
            for cp in copies:
                cp.start()
        else:
            @pl.when(cond)
            def _():
                for cp in copies:
                    cp.start()

    top = zh == 0
    root = top & (y < 2)
    notroot = (zh > 0) | (y >= 2)
    inner = (zh == 1) | (zh == 3)
    high = zl // UPS
    first = at(zh=3 - 2 * high)
    second = at(zh=1 + 2 * high)
    via1, via3 = (zh == 1) & (high == 1), (zh == 3) & (high == 0)

    barrier = pltpu.get_barrier_semaphore()

    @pl.when(top)
    def _():
        for z in (2, 1, 3):
            pl.semaphore_signal(barrier, inc=1, device_id=at(zh=z), device_id_type=MESH)
    for dev in near:
        pl.semaphore_signal(barrier, inc=1, device_id=dev, device_id_type=MESH)

    s_own = sum(bit(j) * (1 << (BITS - 1 - j)) for j in range(BITS))
    own = pan.at[x, c, s_own]
    loads = [pltpu.make_async_copy(piv_hbm, piv, local.at[0]),
             pltpu.make_async_copy(mat_hbm, mat, local.at[1]),
             pltpu.make_async_copy(pan_hbm, own, local.at[2])]
    for cp in loads:
        cp.start()
    loads[0].wait()

    def pack_own(prowv, slot):
        me = (y * ZH + zh) * KC
        kk = lax.broadcasted_iota(I32, (128, NB), 0)
        mine = (kk < KC) & ((kk + me).astype(F32) == slot)
        where_row = jnp.sum(
            jnp.where(mine, (prowv - prow * ROWS + 1).astype(F32), 0.0), axis=1, keepdims=True
        ) - 1.0
        pick = jnp.where(
            lax.broadcasted_iota(I32, (128, ROWS), 1).astype(F32) == where_row, 1.0, 0.0
        ).astype(F32)
        mh, mm, ml = split3(mat[...])
        pick16 = pick[:KC].astype(BF16)
        vloc[...] = (dot(pick16, mh) + dot(pick16, mm)) + dot(pick16, ml)
        scat[...] = jnp.transpose(pick).astype(BF16)

    prowv = piv[...]
    named = prowv >= NB
    group = (prowv // ROWS) % Y * ZH + (prowv // ROWS) // Y
    onehot = jnp.where(
        (lax.broadcasted_iota(I32, (ZH * Y, NB), 0) == group) & named, 1.0, 0.0
    ).astype(F32)
    tri = jnp.where(
        lax.broadcasted_iota(I32, (128, 128), 0) < lax.broadcasted_iota(I32, (128, 128), 1), 1.0, 0.0
    ).astype(BF16)
    before = jnp.zeros((ZH * Y, 1), F32)
    ranks = []
    for b in range(NB // 128):
        part = onehot[:, b * 128:(b + 1) * 128]
        count = dot(part.astype(BF16), tri) + before
        ranks.append(jnp.sum(count * part, axis=0, keepdims=True))
        before = before + jnp.sum(part, axis=1, keepdims=True)
    rank = jnp.concatenate(ranks, axis=1)
    slot = jnp.where(named, group.astype(F32) * KC + rank, -1.0)
    slots[...] = jnp.broadcast_to(slot, (8, NB))

    loads[1].wait()

    @pl.when(root)
    def _():
        vloc[...] = jnp.zeros((KC, COLS), F32)
        tt[y] = mat[...]

    @pl.when(notroot)
    def _():
        pack_own(prowv, slot)
    dme[KC:, :] = jnp.zeros((128 - KC, COLS), F32)

    @pl.when(top)
    def _():
        vall[y, 0] = vloc[...]

    loads[2].wait()
    pl.semaphore_wait(barrier, len(near) + (zh + ZH - 1) // ZH)

    j0 = BITS - 1
    start([rc(own, own, "pz0", zdev[j0])])
    start([rc(vloc, vall.at[y, 1], "v1", down)], zh == 1)
    start([rc(vloc, vall.at[y, 3], "v3", up)], zh == 3)
    start([rc(vloc, vall.at[y, 2], "v2", at(zh=(zh + 2) % ZH))], zh == 2)
    start([rc(mat, tt.at[0], "t0", ydev[1])], top & (y == 0))

    def to_roots(z):
        for d in range(1, Y):
            target = (y + d) % Y
            start([rc(vall.at[y, z], vall.at[y, z], ("vy", d, z), ydev[d])], top & (target < 2))

    to_roots(0)

    def to_core(d, piece, first):
        blocks = pan.at[(x + X - d) % X, c, pl.ds(first, HALF)]
        start([rc(blocks, blocks, ("pc", d, piece), other)])

    def over_x(piece, first):
        blocks = pan.at[x, c, pl.ds(first, HALF)]
        for d in (2, 1, 3):
            start([rc(blocks, blocks, ("px", d, piece), xdev[d])])
        to_core(0, piece, first)

    for t in range(BITS):
        j = BITS - 1 - t
        size = 1 << t
        base_in = (s_own // size) * size
        theirs = base_in + (size - 2 * size * ((s_own // size) % 2))
        arrived(pan.at[x, c, pl.ds(theirs, size)] if t else pan.at[x, c, theirs], ("pz%d" % t))
        if t + 1 < BITS:
            nxt = 2 * size
            have = (s_own // nxt) * nxt
            start([rc(pan.at[x, c, pl.ds(have, nxt)], pan.at[x, c, pl.ds(have, nxt)],
                      "pz%d" % (t + 1), zdev[j - 1])])
        if t + 2 == BITS:
            over_x(0, have)

    over_x(1, theirs)

    @pl.when(root & (y == 1))
    def _():
        arrived(tt.at[0], "t0")

    @pl.when(root)
    def _():
        def tops(i, carry):
            for h in range(2):
                hi, mid, lo = split3(tt[h, pl.ds(i * 128, 128), :])
                at_row = pl.ds(h * ROWS + i * 128, 128)
                thm[at_row, 0:128] = hi
                thm[at_row, 128:256] = mid
                tlo[at_row, :] = lo
            return carry

        @pl.when(y == 0)
        def _():
            tt[1] = jnp.zeros((ROWS, COLS), F32)
        lax.fori_loop(0, ROWS // 128, tops, 0)
        slotc[...] = jnp.transpose(jnp.broadcast_to(slots[0:1, :], (128, NB)))

        def choose(i, carry):
            rows = pl.ds(i * 128, 128)
            lane = lax.broadcasted_iota(I32, (128, 128), 1)
            for b in range(SLOTS // 128):
                sel[rows, b * 128:(b + 1) * 128] = jnp.where(
                    (lane + b * 128).astype(F32) == slotc[rows, :], 1.0, 0.0).astype(BF16)
            return carry
        lax.fori_loop(0, 4 + 4 * y, choose, 0)

    @pl.when(root & (y == 1))
    def _():
        def pack(i, carry):
            ss = lax.broadcasted_iota(I32, (ZH * KC, NB), 0) + i * (ZH * KC)
            got = jnp.where(ss.astype(F32) == slots[0:1, :], 1.0, 0.0).astype(BF16)
            two = dot(got, thm[...])
            all3 = (two[:, :128] + two[:, 128:]) + dot(got, tlo[...])
            for z in range(ZH):
                dall[i, z] = all3[z * KC:(z + 1) * KC]
            return carry
        lax.fori_loop(0, Y, pack, 0)

    for d in range(1, Y):
        start([rc(dall.at[(y + d) % Y], dall.at[(y + d) % Y], "dy", ydev[d])], top & (y == 1))

    for z in (1, 3):
        @pl.when(top)
        def _():
            arrived(vall.at[y, z], "v%d" % z)
        to_roots(z)

    for d in (1, 3, 2):
        src = (x + X - d) % X
        arrived(pan.at[src, c, pl.ds(have, HALF)], ("px", d, 0))
        to_core(d, 0, have)

    @pl.when(top & (y != 1))
    def _():
        arrived(dall.at[y], "dy")
    start([rc(dall.at[y, 1], dme.at[pl.ds(0, KC)], "d", up),
           rc(dall.at[y, 3], dme.at[pl.ds(0, KC)], "d", down)], top)

    for d in (1, 3, 2):
        src = (x + X - d) % X
        arrived(pan.at[src, c, pl.ds(theirs, HALF)], ("px", d, 1))
        to_core(d, 1, theirs)

    @pl.when(top)
    def _():
        arrived(vall.at[y, 2], "v2")
    to_roots(2)
    start([rc(dall.at[y, 2], dfwd, "df", first)], top)

    for piece, mine_at in enumerate((have, theirs)):
        for d in range(X):
            arrived(pan.at[(x + X - d) % X, 1 - c, pl.ds(mine_at, HALF)], ("pc", d, piece))

    def psplit(i, carry):
        for cc in range(C):
            for s in range(ZL):
                hi, lo = split(pan[i, cc, s])
                rows = pl.ds((cc * ZL + s) * BLK, BLK)
                for q, line in enumerate(NATURAL):
                    phi[i, rows, line * QR:(line + 1) * QR] = hi[:, q * QR:(q + 1) * QR]
                    plo[i, rows, line * QR:(line + 1) * QR] = lo[:, q * QR:(q + 1) * QR]
        return carry
    lax.fori_loop(0, X, psplit, 0)

    @pl.when(root)
    def _():
        for d in range(1, Y):
            src = (y + Y - d) % Y
            for z in range(ZH):
                arrived(vall.at[src, z], ("vy", d, z))

        def vsplit(i, carry):
            for z in range(ZH):
                hi, lo = split(vall[i, z])
                vhl[pl.ds(i * (ZH * KC) + z * KC, KC), 0:128] = hi
                vhl[pl.ds(i * (ZH * KC) + z * KC, KC), 128:256] = lo
            return carry
        lax.fori_loop(0, Y, vsplit, 0)

        def form(i, q, line):
            rows = pl.ds(q * QR + i * 128, 128)
            sc = slotc[rows, :]
            moved = dot(sel[rows, :], vhl[...])
            stay = jnp.concatenate([sc, sc], axis=1) < 0.0
            phl[pl.ds(line * QR + i * 128, 128), :] = jnp.where(
                stay, thm[rows, :].astype(F32), moved).astype(BF16)

        def form_two(q, line):
            def body(i, carry):
                form(i, q, line)
                return carry
            lax.fori_loop(0, 2, body, 0)

        form_two(0, NATURAL[0])
        form_two(1, NATURAL[1])

        @pl.when(y == 0)
        def _():
            for line in NATURAL[2:]:
                phl[line * QR:(line + 1) * QR, :] = jnp.zeros((QR, 2 * COLS), BF16)

        @pl.when(y == 1)
        def _():
            form_two(2, NATURAL[2])
            form_two(3, NATURAL[3])

    def blocks(i, right, store, cols=slice(None)):
        two = dot(phi[i, :, cols], right[...])
        res = (two[:, :128] + two[:, 128:]) + dot(plo[i, :, cols], right[:, 0:128])
        for cc in range(C):
            for s in range(ZL):
                k = cc * ZL + s
                store(i * TILE + BLK * (rev(s) * C + cc), res[k * BLK:(k + 1) * BLK])

    def u_tile(i):
        h = i // 2
        line = y + h * (3 - 2 * y)

        @pl.when(root)
        def _():
            def store(row, val):
                ub[line, pl.ds(row - h * QR, BLK), :] = val
                out[pl.ds(row, BLK), :] = val
            blocks(i, phl, store)

    def chunk(line, k):
        return ub.at[line, pl.ds(k * CH, CH)]

    def ukey(rel, k):
        return ("u", rel, k)

    def send_chunk(line, rel, k, dev, cond):
        start([rc(chunk(line, k), chunk(line, k), ukey(rel, k), dev)], cond)

    firsts = [rc(chunk(y, k), chunk(y, k), ukey(0, k), first) for k in range(NCH)]

    def send_first(k, cond):
        @pl.when(cond)
        def _():
            firsts[k].start()

    r0, r1 = top & (y == 0), top & (y == 1)
    per = TILE // CH
    for i in (2, 3, 0, 1):
        u_tile(i)
        for k in range((i % 2) * per, (i % 2 + 1) * per):
            if i >= 2:
                send_chunk(3, 0, k, ydev[3], r0)
                send_chunk(2, 0, k, ydev[1], r1)
            else:
                send_first(k, root & (zl != MIDDLE))
    for k in range(NCH):
        send_chunk(3, 1, k, ydev[2], r0)
        send_chunk(0, 2, k, ydev[2], r0)
        send_chunk(0, 1, k, ydev[3], r0)
        send_chunk(1, 3, k, ydev[1], r1)
        send_chunk(1, 2, k, ydev[2], r1)
        send_chunk(2, 3, k, ydev[2], r1)

    nonroot = top & (y >= 2)
    for k in range(NCH):
        @pl.when(nonroot)
        def _():
            arrived(chunk(y, k), ukey(0, k))
        send_first(k, nonroot & (zl != MIDDLE))

    @pl.when(top & (zl == MIDDLE))
    def _():
        pl.semaphore_wait(token.at[1], 1)
        for cp in firsts:
            cp.start()

    @pl.when(top)
    def _():
        @pl.when(zl == ZL - 1)
        def _():
            for q in range(MIDDLE, -1, -1):
                pl.semaphore_signal(token.at[0], inc=1, device_id=at(zl=q), device_id_type=MESH)
        for k in range(NCH // 2):
            firsts[k].wait_send()

        @pl.when(zl == 0)
        def _():
            for q in range(MIDDLE, ZL):
                pl.semaphore_signal(token.at[1], inc=1, device_id=at(zl=q), device_id_type=MESH)
        for k in range(NCH // 2, NCH):
            firsts[k].wait_send()

        @pl.when(zl <= MIDDLE)
        def _():
            pl.semaphore_wait(token.at[0], 1)

        @pl.when(zl > MIDDLE)
        def _():
            pl.semaphore_wait(token.at[1], 1)
    for k in range(NCH):
        send_chunk(y, 0, k, second, top)

    @pl.when(via1 | via3)
    def _():
        arrived(dfwd, "df")
    start([rc(dfwd, dme.at[pl.ds(0, KC)], "d", up)], via1)
    start([rc(dfwd, dme.at[pl.ds(0, KC)], "d", down)], via3)

    @pl.when(nonroot)
    def _():
        dme[0:KC, :] = dall[y, 0]

    @pl.when(zh > 0)
    def _():
        arrived(dme.at[pl.ds(0, KC)], "d")

    @pl.when(notroot)
    def _():
        hit = jnp.sum(scat[...].astype(F32), axis=1, keepdims=True) > 0.0
        dh, dm, dl = split3(dme[...])
        moved = (dot(scat[...], dh) + dot(scat[...], dm)) + dot(scat[...], dl)
        base[...] = jnp.where(hit, moved, mat[...])

    for k in range(NCH):
        @pl.when(zh > 0)
        def _():
            arrived(chunk(y, k), ukey(0, k))
        send_chunk(y, 0, k, up, via1)
        send_chunk(y, 0, k, down, via3)
        for d in (2, 1, 3):
            send_chunk(y, Y - d, k, ydev[d], zh > 0)

    @pl.when(notroot)
    def _():
        def line_step(line, last):
            hi, lo = split(ub[line])
            uhl[:, 0:128] = hi
            uhl[:, 128:256] = lo
            at_col = pl.ds(pl.multiple_of(line * QR, QR), QR)

            def store(row, val):
                rows = pl.ds(row, BLK)
                if last:
                    out[rows, :] = base[rows, :] - val
                else:
                    base[rows, :] = base[rows, :] - val

            for i in range(X):
                blocks(i, uhl, store, at_col)

        line_step(y, False)
        for rel in (1, 3, 2):
            for k in range(NCH):
                arrived(chunk((y + rel) % Y, k), ukey(rel, k))
            line_step((y + rel) % Y, rel == 2)

    for cond, copies in pending:
        if cond is None:
            for cp in copies:
                cp.wait_send()
        else:
            @pl.when(cond)
            def _(copies=copies):
                for cp in copies:
                    cp.wait_send()


def per_device(matrix, panel, pivots):
    hbm, vmem = pl.BlockSpec(memory_space=pltpu.HBM), pl.BlockSpec(memory_space=pltpu.VMEM)
    return pl.pallas_call(
        kernel,
        out_shape=jax.ShapeDtypeStruct((ROWS, COLS), F32),
        in_specs=[hbm] * 3,
        out_specs=vmem,
        scratch_shapes=[
            pltpu.VMEM((ROWS, COLS), F32),
            pltpu.VMEM((1, NB), I32),
            pltpu.VMEM((X, C, ZL, BLK, NB), F32),
            pltpu.VMEM((X, TILE, NB), BF16),
            pltpu.VMEM((X, TILE, NB), BF16),
            pltpu.VMEM((KC, COLS), F32),
            pltpu.VMEM((Y, ZH, KC, COLS), F32),
            pltpu.VMEM((SLOTS, 2 * COLS), BF16),
            pltpu.VMEM((2, ROWS, COLS), F32),
            pltpu.VMEM((NB, 2 * COLS), BF16),
            pltpu.VMEM((NB, COLS), BF16),
            pltpu.VMEM((8, NB), F32),
            pltpu.VMEM((NB, 128), F32),
            pltpu.VMEM((NB, 2 * COLS), BF16),
            pltpu.VMEM((Y, ZH, KC, COLS), F32),
            pltpu.VMEM((128, COLS), F32),
            pltpu.VMEM((KC, COLS), F32),
            pltpu.VMEM((ROWS, 128), BF16),
            pltpu.VMEM((NB, SLOTS), BF16),
            pltpu.VMEM((ROWS, COLS), F32),
            pltpu.VMEM((4, ROWS // 2, COLS), F32),
            pltpu.VMEM((QR, 2 * COLS), BF16),
            pltpu.SemaphoreType.DMA((192,)),
            pltpu.SemaphoreType.DMA((64,)),
            pltpu.SemaphoreType.DMA((3,)),
            pltpu.SemaphoreType.REGULAR((2,)),
        ],
        compiler_params=pltpu.CompilerParams(
            collective_id=0, has_side_effects=True, vmem_limit_bytes=40 * 2**20
        ),
    )(matrix, panel, pivots.reshape(1, NB))


def solution(mesh):
    placed = (P("prow", "pcol"), P(("prow", "pcol"), None), P())
    return jax.shard_map(
        per_device, mesh=mesh, in_specs=placed, out_specs=P("prow", "pcol"), check_vma=False
    )
```

```python
import jax
import jax.numpy as jnp
from jax import lax
from jax.experimental import pallas as pl
from jax.experimental.pallas import tpu as pltpu
from jax.sharding import PartitionSpec as P

MESH = pl.DeviceIdType.MESH
F32, BF16, I32 = jnp.float32, jnp.bfloat16, jnp.int32

ZH, Y, X, ZL, C = 4, 4, 4, 8, 2
ROWS, NB, COLS = 512, 1024, 128
BLK = ROWS // (X * ZL * C)
KC = 48
SLOTS = ZH * Y * KC
CH, NCH = 64, 4
TILE = ROWS // X
NATURAL = (0, 3, 1, 2)
BITS = ZL.bit_length() - 1
HALF = ZL // 2
QR = NB // 4


def rev(s):
    return sum(((s >> j) & 1) << (BITS - 1 - j) for j in range(BITS))


def dot(a, b):
    return jnp.dot(a, b, preferred_element_type=F32)


def split(a):
    hi = a.astype(BF16)
    return hi, (a - hi.astype(F32)).astype(BF16)


def split3(a):
    hi = a.astype(BF16)
    rest = a - hi.astype(F32)
    mid = rest.astype(BF16)
    return hi, mid, (rest - mid.astype(F32)).astype(BF16)


def kernel(
    mat_hbm, pan_hbm, piv_hbm, out,
    mat, piv, pan, phi, plo, vloc, vall, vhl, tt, thm, tlo, slots, slotc, phl,
    dall, dme, dfwd, scat, sel, base, ub, uhl, send, recv, local, token,
):
    prow, pcol = lax.axis_index("prow"), lax.axis_index("pcol")
    zh, y = prow // Y, prow % Y
    x, zl, c = pcol // (ZL * C), (pcol // C) % ZL, pcol % C

    def at(zh=zh, y=y, x=x, zl=zl, c=c):
        return (zh * Y + y, x * (ZL * C) + zl * C + c)

    def bit(j):
        return (zl // (1 << j)) % 2

    ydev = [at(y=(y + d) % Y) for d in range(Y)]
    xdev = [at(x=(x + d) % X) for d in range(X)]
    zdev = [at(zl=zl + (1 << j) - (2 << j) * bit(j)) for j in range(BITS)]
    other = at(c=1 - c)
    up, down = at(zh=(zh + 1) % ZH), at(zh=(zh + ZH - 1) % ZH)
    near = ydev[1:] + xdev[1:] + zdev + [other]

    names = {}

    def num(key):
        return names.setdefault(key, len(names))

    counter = [0]

    def rc(src, dst, key, dev):
        sid = counter[0]
        counter[0] += 1
        return pltpu.make_async_remote_copy(
            src_ref=src, dst_ref=dst, send_sem=send.at[sid], recv_sem=recv.at[num(key)],
            device_id=dev, device_id_type=MESH,
        )

    def arrived(dst, key):
        pltpu.make_async_remote_copy(
            src_ref=dst, dst_ref=dst, send_sem=send.at[0], recv_sem=recv.at[num(key)],
            device_id=other, device_id_type=MESH,
        ).wait_recv()

    pending = []

    def start(copies, cond=None):
        pending.append((cond, copies))
        if cond is None:
            for cp in copies:
                cp.start()
        else:
            @pl.when(cond)
            def _():
                for cp in copies:
                    cp.start()

    top = zh == 0
    root = top & (y < 2)
    notroot = (zh > 0) | (y >= 2)
    inner = (zh == 1) | (zh == 3)
    low = zl // (ZL // 2)
    first = at(zh=3 - 2 * low)
    second = at(zh=1 + 2 * low)
    via1, via3 = (zh == 1) & (low == 1), (zh == 3) & (low == 0)

    barrier = pltpu.get_barrier_semaphore()

    @pl.when(top)
    def _():
        for z in (2, 1, 3):
            pl.semaphore_signal(barrier, inc=1, device_id=at(zh=z), device_id_type=MESH)
    for dev in near:
        pl.semaphore_signal(barrier, inc=1, device_id=dev, device_id_type=MESH)

    s_own = sum(bit(j) * (1 << (BITS - 1 - j)) for j in range(BITS))
    own = pan.at[x, c, s_own]
    loads = [pltpu.make_async_copy(piv_hbm, piv, local.at[0]),
             pltpu.make_async_copy(mat_hbm, mat, local.at[1]),
             pltpu.make_async_copy(pan_hbm, own, local.at[2])]
    for cp in loads:
        cp.start()
    loads[0].wait()

    def pack_own(prowv, slot):
        me = (y * ZH + zh) * KC
        kk = lax.broadcasted_iota(I32, (128, NB), 0)
        mine = (kk < KC) & ((kk + me).astype(F32) == slot)
        where_row = jnp.sum(
            jnp.where(mine, (prowv - prow * ROWS + 1).astype(F32), 0.0), axis=1, keepdims=True
        ) - 1.0
        pick = jnp.where(
            lax.broadcasted_iota(I32, (128, ROWS), 1).astype(F32) == where_row, 1.0, 0.0
        ).astype(F32)
        mh, mm, ml = split3(mat[...])
        pick16 = pick[:KC].astype(BF16)
        vloc[...] = (dot(pick16, mh) + dot(pick16, mm)) + dot(pick16, ml)
        scat[...] = jnp.transpose(pick).astype(BF16)

    prowv = piv[...]
    named = prowv >= NB
    group = (prowv // ROWS) % Y * ZH + (prowv // ROWS) // Y
    onehot = jnp.where(
        (lax.broadcasted_iota(I32, (ZH * Y, NB), 0) == group) & named, 1.0, 0.0
    ).astype(F32)
    tri = jnp.where(
        lax.broadcasted_iota(I32, (128, 128), 0) < lax.broadcasted_iota(I32, (128, 128), 1), 1.0, 0.0
    ).astype(BF16)
    before = jnp.zeros((ZH * Y, 1), F32)
    ranks = []
    for b in range(NB // 128):
        part = onehot[:, b * 128:(b + 1) * 128]
        count = dot(part.astype(BF16), tri) + before
        ranks.append(jnp.sum(count * part, axis=0, keepdims=True))
        before = before + jnp.sum(part, axis=1, keepdims=True)
    rank = jnp.concatenate(ranks, axis=1)
    slot = jnp.where(named, group.astype(F32) * KC + rank, -1.0)
    slots[...] = jnp.broadcast_to(slot, (8, NB))

    loads[1].wait()

    @pl.when(root)
    def _():
        vloc[...] = jnp.zeros((KC, COLS), F32)
        tt[y] = mat[...]

    @pl.when(notroot)
    def _():
        pack_own(prowv, slot)
    dme[KC:, :] = jnp.zeros((128 - KC, COLS), F32)

    @pl.when(top)
    def _():
        vall[y, 0] = vloc[...]

    loads[2].wait()
    pl.semaphore_wait(barrier, len(near) + (zh + ZH - 1) // ZH)

    j0 = BITS - 1
    start([rc(own, own, "pz0", zdev[j0])])
    start([rc(vloc, vall.at[y, 1], "v1", down)], zh == 1)
    start([rc(vloc, vall.at[y, 3], "v3", up)], zh == 3)
    start([rc(vloc, vall.at[y, 2], "v2", at(zh=(zh + 2) % ZH))], zh == 2)
    start([rc(mat, tt.at[0], "t0", ydev[1])], top & (y == 0))

    def to_roots(z):
        for d in range(1, Y):
            target = (y + d) % Y
            start([rc(vall.at[y, z], vall.at[y, z], ("vy", d, z), ydev[d])], top & (target < 2))

    to_roots(0)

    def to_core(d, piece, first):
        blocks = pan.at[(x + X - d) % X, c, pl.ds(first, HALF)]
        start([rc(blocks, blocks, ("pc", d, piece), other)])

    def over_x(piece, first):
        blocks = pan.at[x, c, pl.ds(first, HALF)]
        for d in (2, 1, 3):
            start([rc(blocks, blocks, ("px", d, piece), xdev[d])])
        to_core(0, piece, first)

    for t in range(BITS):
        j = BITS - 1 - t
        size = 1 << t
        base_in = (s_own // size) * size
        theirs = base_in + (size - 2 * size * ((s_own // size) % 2))
        arrived(pan.at[x, c, pl.ds(theirs, size)] if t else pan.at[x, c, theirs], ("pz%d" % t))
        if t + 1 < BITS:
            nxt = 2 * size
            have = (s_own // nxt) * nxt
            start([rc(pan.at[x, c, pl.ds(have, nxt)], pan.at[x, c, pl.ds(have, nxt)],
                      "pz%d" % (t + 1), zdev[j - 1])])
        if t + 2 == BITS:
            over_x(0, have)

    over_x(1, theirs)

    @pl.when(root & (y == 1))
    def _():
        arrived(tt.at[0], "t0")

    @pl.when(root)
    def _():
        def tops(i, carry):
            for h in range(2):
                hi, mid, lo = split3(tt[h, pl.ds(i * 128, 128), :])
                at_row = pl.ds(h * ROWS + i * 128, 128)
                thm[at_row, 0:128] = hi
                thm[at_row, 128:256] = mid
                tlo[at_row, :] = lo
            return carry

        @pl.when(y == 0)
        def _():
            tt[1] = jnp.zeros((ROWS, COLS), F32)
        lax.fori_loop(0, ROWS // 128, tops, 0)
        slotc[...] = jnp.transpose(jnp.broadcast_to(slots[0:1, :], (128, NB)))

        def choose(i, carry):
            rows = pl.ds(i * 128, 128)
            lane = lax.broadcasted_iota(I32, (128, 128), 1)
            for b in range(SLOTS // 128):
                sel[rows, b * 128:(b + 1) * 128] = jnp.where(
                    (lane + b * 128).astype(F32) == slotc[rows, :], 1.0, 0.0).astype(BF16)
            return carry
        lax.fori_loop(0, 4 + 4 * y, choose, 0)

    @pl.when(root & (y == 1))
    def _():
        def pack(i, carry):
            ss = lax.broadcasted_iota(I32, (ZH * KC, NB), 0) + i * (ZH * KC)
            got = jnp.where(ss.astype(F32) == slots[0:1, :], 1.0, 0.0).astype(BF16)
            two = dot(got, thm[...])
            all3 = (two[:, :128] + two[:, 128:]) + dot(got, tlo[...])
            for z in range(ZH):
                dall[i, z] = all3[z * KC:(z + 1) * KC]
            return carry
        lax.fori_loop(0, Y, pack, 0)

    for d in range(1, Y):
        start([rc(dall.at[(y + d) % Y], dall.at[(y + d) % Y], "dy", ydev[d])], top & (y == 1))

    for z in (1, 3):
        @pl.when(top)
        def _():
            arrived(vall.at[y, z], "v%d" % z)
        to_roots(z)

    for d in (1, 3, 2):
        src = (x + X - d) % X
        arrived(pan.at[src, c, pl.ds(have, HALF)], ("px", d, 0))
        to_core(d, 0, have)

    @pl.when(top & (y != 1))
    def _():
        arrived(dall.at[y], "dy")
    start([rc(dall.at[y, 1], dme.at[pl.ds(0, KC)], "d", up),
           rc(dall.at[y, 3], dme.at[pl.ds(0, KC)], "d", down)], top)

    for d in (1, 3, 2):
        src = (x + X - d) % X
        arrived(pan.at[src, c, pl.ds(theirs, HALF)], ("px", d, 1))
        to_core(d, 1, theirs)

    @pl.when(top)
    def _():
        arrived(vall.at[y, 2], "v2")
    to_roots(2)
    start([rc(dall.at[y, 2], dfwd, "df", first)], top)

    for piece, mine_at in enumerate((have, theirs)):
        for d in range(X):
            arrived(pan.at[(x + X - d) % X, 1 - c, pl.ds(mine_at, HALF)], ("pc", d, piece))

    def psplit(i, carry):
        for cc in range(C):
            for s in range(ZL):
                hi, lo = split(pan[i, cc, s])
                rows = pl.ds((cc * ZL + s) * BLK, BLK)
                for q, line in enumerate(NATURAL):
                    phi[i, rows, line * QR:(line + 1) * QR] = hi[:, q * QR:(q + 1) * QR]
                    plo[i, rows, line * QR:(line + 1) * QR] = lo[:, q * QR:(q + 1) * QR]
        return carry
    lax.fori_loop(0, X, psplit, 0)

    @pl.when(root)
    def _():
        for d in range(1, Y):
            src = (y + Y - d) % Y
            for z in range(ZH):
                arrived(vall.at[src, z], ("vy", d, z))

        def vsplit(i, carry):
            for z in range(ZH):
                hi, lo = split(vall[i, z])
                vhl[pl.ds(i * (ZH * KC) + z * KC, KC), 0:128] = hi
                vhl[pl.ds(i * (ZH * KC) + z * KC, KC), 128:256] = lo
            return carry
        lax.fori_loop(0, Y, vsplit, 0)

        def form(i, q, line):
            rows = pl.ds(q * QR + i * 128, 128)
            sc = slotc[rows, :]
            moved = dot(sel[rows, :], vhl[...])
            stay = jnp.concatenate([sc, sc], axis=1) < 0.0
            phl[pl.ds(line * QR + i * 128, 128), :] = jnp.where(
                stay, thm[rows, :].astype(F32), moved).astype(BF16)

        def form_two(q, line):
            def body(i, carry):
                form(i, q, line)
                return carry
            lax.fori_loop(0, 2, body, 0)

        form_two(0, NATURAL[0])
        form_two(1, NATURAL[1])

        @pl.when(y == 0)
        def _():
            for line in NATURAL[2:]:
                phl[line * QR:(line + 1) * QR, :] = jnp.zeros((QR, 2 * COLS), BF16)

        @pl.when(y == 1)
        def _():
            form_two(2, NATURAL[2])
            form_two(3, NATURAL[3])

    def blocks(i, right, store, cols=slice(None)):
        two = dot(phi[i, :, cols], right[...])
        res = (two[:, :128] + two[:, 128:]) + dot(plo[i, :, cols], right[:, 0:128])
        for cc in range(C):
            for s in range(ZL):
                k = cc * ZL + s
                store(i * TILE + BLK * (rev(s) * C + cc), res[k * BLK:(k + 1) * BLK])

    def u_tile(i):
        h = i // 2
        line = y + h * (3 - 2 * y)

        @pl.when(root)
        def _():
            def store(row, val):
                ub[line, pl.ds(row - h * QR, BLK), :] = val
                out[pl.ds(row, BLK), :] = val
            blocks(i, phl, store)

    def chunk(line, k):
        return ub.at[line, pl.ds(k * CH, CH)]

    def ukey(rel, k):
        return ("u", rel, k)

    def send_chunk(line, rel, k, dev, cond):
        start([rc(chunk(line, k), chunk(line, k), ukey(rel, k), dev)], cond)

    firsts = [rc(chunk(y, k), chunk(y, k), ukey(0, k), first) for k in range(NCH)]

    def send_first(k, cond):
        @pl.when(cond)
        def _():
            firsts[k].start()

    r0, r1 = top & (y == 0), top & (y == 1)
    per = TILE // CH
    for i in (2, 3, 0, 1):
        u_tile(i)
        for k in range((i % 2) * per, (i % 2 + 1) * per):
            if i >= 2:
                send_chunk(3, 0, k, ydev[3], r0)
                send_chunk(2, 0, k, ydev[1], r1)
            else:
                send_first(k, root)
    for k in range(NCH):
        send_chunk(3, 1, k, ydev[2], r0)
        send_chunk(0, 2, k, ydev[2], r0)
        send_chunk(0, 1, k, ydev[3], r0)
        send_chunk(1, 3, k, ydev[1], r1)
        send_chunk(1, 2, k, ydev[2], r1)
        send_chunk(2, 3, k, ydev[2], r1)

    nonroot = top & (y >= 2)
    for k in range(NCH):
        @pl.when(nonroot)
        def _():
            arrived(chunk(y, k), ukey(0, k))
        send_first(k, nonroot)

    @pl.when(top)
    def _():
        for cp in firsts:
            cp.wait_send()
        pl.semaphore_signal(token, inc=1, device_id=zdev[BITS - 1], device_id_type=MESH)
        pl.semaphore_wait(token, 1)
    for k in range(NCH):
        send_chunk(y, 0, k, second, top)

    @pl.when(via1 | via3)
    def _():
        arrived(dfwd, "df")
    start([rc(dfwd, dme.at[pl.ds(0, KC)], "d", up)], via1)
    start([rc(dfwd, dme.at[pl.ds(0, KC)], "d", down)], via3)

    @pl.when(nonroot)
    def _():
        dme[0:KC, :] = dall[y, 0]

    @pl.when(zh > 0)
    def _():
        arrived(dme.at[pl.ds(0, KC)], "d")

    @pl.when(notroot)
    def _():
        hit = jnp.sum(scat[...].astype(F32), axis=1, keepdims=True) > 0.0
        dh, dm, dl = split3(dme[...])
        moved = (dot(scat[...], dh) + dot(scat[...], dm)) + dot(scat[...], dl)
        base[...] = jnp.where(hit, moved, mat[...])

    for k in range(NCH):
        @pl.when(zh > 0)
        def _():
            arrived(chunk(y, k), ukey(0, k))
        send_chunk(y, 0, k, up, via1)
        send_chunk(y, 0, k, down, via3)
        for d in (2, 1, 3):
            send_chunk(y, Y - d, k, ydev[d], zh > 0)

    @pl.when(notroot)
    def _():
        def line_step(line, last):
            hi, lo = split(ub[line])
            uhl[:, 0:128] = hi
            uhl[:, 128:256] = lo
            at_col = pl.ds(pl.multiple_of(line * QR, QR), QR)

            def store(row, val):
                rows = pl.ds(row, BLK)
                if last:
                    out[rows, :] = base[rows, :] - val
                else:
                    base[rows, :] = base[rows, :] - val

            for i in range(X):
                blocks(i, uhl, store, at_col)

        line_step(y, False)
        for rel in (1, 3, 2):
            for k in range(NCH):
                arrived(chunk((y + rel) % Y, k), ukey(rel, k))
            line_step((y + rel) % Y, rel == 2)

    for cond, copies in pending:
        if cond is None:
            for cp in copies:
                cp.wait_send()
        else:
            @pl.when(cond)
            def _(copies=copies):
                for cp in copies:
                    cp.wait_send()


def per_device(matrix, panel, pivots):
    hbm, vmem = pl.BlockSpec(memory_space=pltpu.HBM), pl.BlockSpec(memory_space=pltpu.VMEM)
    return pl.pallas_call(
        kernel,
        out_shape=jax.ShapeDtypeStruct((ROWS, COLS), F32),
        in_specs=[hbm] * 3,
        out_specs=vmem,
        scratch_shapes=[
            pltpu.VMEM((ROWS, COLS), F32),
            pltpu.VMEM((1, NB), I32),
            pltpu.VMEM((X, C, ZL, BLK, NB), F32),
            pltpu.VMEM((X, TILE, NB), BF16),
            pltpu.VMEM((X, TILE, NB), BF16),
            pltpu.VMEM((KC, COLS), F32),
            pltpu.VMEM((Y, ZH, KC, COLS), F32),
            pltpu.VMEM((SLOTS, 2 * COLS), BF16),
            pltpu.VMEM((2, ROWS, COLS), F32),
            pltpu.VMEM((NB, 2 * COLS), BF16),
            pltpu.VMEM((NB, COLS), BF16),
            pltpu.VMEM((8, NB), F32),
            pltpu.VMEM((NB, 128), F32),
            pltpu.VMEM((NB, 2 * COLS), BF16),
            pltpu.VMEM((Y, ZH, KC, COLS), F32),
            pltpu.VMEM((128, COLS), F32),
            pltpu.VMEM((KC, COLS), F32),
            pltpu.VMEM((ROWS, 128), BF16),
            pltpu.VMEM((NB, SLOTS), BF16),
            pltpu.VMEM((ROWS, COLS), F32),
            pltpu.VMEM((4, ROWS // 2, COLS), F32),
            pltpu.VMEM((QR, 2 * COLS), BF16),
            pltpu.SemaphoreType.DMA((192,)),
            pltpu.SemaphoreType.DMA((64,)),
            pltpu.SemaphoreType.DMA((3,)),
            pltpu.SemaphoreType.REGULAR,
        ],
        compiler_params=pltpu.CompilerParams(
            collective_id=0, has_side_effects=True, vmem_limit_bytes=40 * 2**20
        ),
    )(matrix, panel, pivots.reshape(1, NB))


def solution(mesh):
    placed = (P("prow", "pcol"), P(("prow", "pcol"), None), P())
    return jax.shard_map(
        per_device, mesh=mesh, in_specs=placed, out_specs=P("prow", "pcol"), check_vma=False
    )
```

```python
import jax
import jax.numpy as jnp
from jax import lax
from jax.experimental import pallas as pl
from jax.experimental.pallas import tpu as pltpu
from jax.sharding import PartitionSpec as P

MESH = pl.DeviceIdType.MESH
F32, BF16, I32 = jnp.float32, jnp.bfloat16, jnp.int32

ZH, Y, X, ZL, C = 4, 4, 4, 8, 2
ROWS, NB, COLS = 512, 1024, 128
BLK = ROWS // (X * ZL * C)
KC = 48
SLOTS = ZH * Y * KC
CH, NCH = 64, 4
TILE = ROWS // X
NATURAL = (0, 3, 1, 2)
BITS = ZL.bit_length() - 1
HALF = ZL // 2
QR = NB // 4


def rev(s):
    return sum(((s >> j) & 1) << (BITS - 1 - j) for j in range(BITS))


def dot(a, b):
    return jnp.dot(a, b, preferred_element_type=F32)


def split(a):
    hi = a.astype(BF16)
    return hi, (a - hi.astype(F32)).astype(BF16)


def split3(a):
    hi = a.astype(BF16)
    rest = a - hi.astype(F32)
    mid = rest.astype(BF16)
    return hi, mid, (rest - mid.astype(F32)).astype(BF16)


def kernel(
    mat_hbm, pan_hbm, piv_hbm, out,
    mat, piv, pan, phi, plo, vloc, vall, vhl, tt, thm, tlo, slots, slotc, phl,
    dall, dme, dfwd, scat, sel, base, ub, uhl, send, recv, local, token,
):
    prow, pcol = lax.axis_index("prow"), lax.axis_index("pcol")
    zh, y = prow // Y, prow % Y
    x, zl, c = pcol // (ZL * C), (pcol // C) % ZL, pcol % C

    def at(zh=zh, y=y, x=x, zl=zl, c=c):
        return (zh * Y + y, x * (ZL * C) + zl * C + c)

    def bit(j):
        return (zl // (1 << j)) % 2

    ydev = [at(y=(y + d) % Y) for d in range(Y)]
    xdev = [at(x=(x + d) % X) for d in range(X)]
    zdev = [at(zl=zl + (1 << j) - (2 << j) * bit(j)) for j in range(BITS)]
    other = at(c=1 - c)
    up, down = at(zh=(zh + 1) % ZH), at(zh=(zh + ZH - 1) % ZH)
    near = ydev[1:] + xdev[1:] + zdev + [other]

    names = {}

    def num(key):
        return names.setdefault(key, len(names))

    counter = [0]

    def rc(src, dst, key, dev):
        sid = counter[0]
        counter[0] += 1
        return pltpu.make_async_remote_copy(
            src_ref=src, dst_ref=dst, send_sem=send.at[sid], recv_sem=recv.at[num(key)],
            device_id=dev, device_id_type=MESH,
        )

    def arrived(dst, key):
        pltpu.make_async_remote_copy(
            src_ref=dst, dst_ref=dst, send_sem=send.at[0], recv_sem=recv.at[num(key)],
            device_id=other, device_id_type=MESH,
        ).wait_recv()

    pending = []

    def start(copies, cond=None):
        pending.append((cond, copies))
        if cond is None:
            for cp in copies:
                cp.start()
        else:
            @pl.when(cond)
            def _():
                for cp in copies:
                    cp.start()

    top = zh == 0
    root = top & (y < 2)
    notroot = (zh > 0) | (y >= 2)
    inner = (zh == 1) | (zh == 3)
    low = zl // (ZL // 2)
    first = at(zh=3 - 2 * low)
    second = at(zh=1 + 2 * low)
    via1, via3 = (zh == 1) & (low == 1), (zh == 3) & (low == 0)

    barrier = pltpu.get_barrier_semaphore()

    @pl.when(top)
    def _():
        for z in (2, 1, 3):
            pl.semaphore_signal(barrier, inc=1, device_id=at(zh=z), device_id_type=MESH)
    for dev in near:
        pl.semaphore_signal(barrier, inc=1, device_id=dev, device_id_type=MESH)

    s_own = sum(bit(j) * (1 << (BITS - 1 - j)) for j in range(BITS))
    own = pan.at[x, c, s_own]
    loads = [pltpu.make_async_copy(piv_hbm, piv, local.at[0]),
             pltpu.make_async_copy(mat_hbm, mat, local.at[1]),
             pltpu.make_async_copy(pan_hbm, own, local.at[2])]
    for cp in loads:
        cp.start()
    loads[0].wait()

    def pack_own(prowv, slot):
        me = (y * ZH + zh) * KC
        kk = lax.broadcasted_iota(I32, (128, NB), 0)
        mine = (kk < KC) & ((kk + me).astype(F32) == slot)
        where_row = jnp.sum(
            jnp.where(mine, (prowv - prow * ROWS + 1).astype(F32), 0.0), axis=1, keepdims=True
        ) - 1.0
        pick = jnp.where(
            lax.broadcasted_iota(I32, (128, ROWS), 1).astype(F32) == where_row, 1.0, 0.0
        ).astype(F32)
        mh, mm, ml = split3(mat[...])
        pick16 = pick[:KC].astype(BF16)
        vloc[...] = (dot(pick16, mh) + dot(pick16, mm)) + dot(pick16, ml)
        scat[...] = jnp.transpose(pick).astype(BF16)

    prowv = piv[...]
    named = prowv >= NB
    group = (prowv // ROWS) % Y * ZH + (prowv // ROWS) // Y
    onehot = jnp.where(
        (lax.broadcasted_iota(I32, (ZH * Y, NB), 0) == group) & named, 1.0, 0.0
    ).astype(F32)
    tri = jnp.where(
        lax.broadcasted_iota(I32, (128, 128), 0) < lax.broadcasted_iota(I32, (128, 128), 1), 1.0, 0.0
    ).astype(BF16)
    before = jnp.zeros((ZH * Y, 1), F32)
    ranks = []
    for b in range(NB // 128):
        part = onehot[:, b * 128:(b + 1) * 128]
        count = dot(part.astype(BF16), tri) + before
        ranks.append(jnp.sum(count * part, axis=0, keepdims=True))
        before = before + jnp.sum(part, axis=1, keepdims=True)
    rank = jnp.concatenate(ranks, axis=1)
    slot = jnp.where(named, group.astype(F32) * KC + rank, -1.0)
    slots[...] = jnp.broadcast_to(slot, (8, NB))

    loads[1].wait()

    @pl.when(root)
    def _():
        vloc[...] = jnp.zeros((KC, COLS), F32)
        tt[y] = mat[...]

    @pl.when(notroot)
    def _():
        pack_own(prowv, slot)
    dme[KC:, :] = jnp.zeros((128 - KC, COLS), F32)

    @pl.when(top)
    def _():
        vall[y, 0] = vloc[...]

    loads[2].wait()
    pl.semaphore_wait(barrier, len(near) + (zh + ZH - 1) // ZH)

    j0 = BITS - 1
    start([rc(own, own, "pz0", zdev[j0])])
    start([rc(vloc, vall.at[y, 1], "v1", down)], zh == 1)
    start([rc(vloc, vall.at[y, 3], "v3", up)], zh == 3)
    start([rc(vloc, vall.at[y, 2], "v2", at(zh=(zh + 2) % ZH))], zh == 2)
    start([rc(mat, tt.at[0], "t0", ydev[1])], top & (y == 0))

    def to_roots(z):
        for d in range(1, Y):
            target = (y + d) % Y
            start([rc(vall.at[y, z], vall.at[y, z], ("vy", d, z), ydev[d])], top & (target < 2))

    to_roots(0)

    def to_core(d, piece, first):
        blocks = pan.at[(x + X - d) % X, c, pl.ds(first, HALF)]
        start([rc(blocks, blocks, ("pc", d, piece), other)])

    def over_x(piece, first):
        blocks = pan.at[x, c, pl.ds(first, HALF)]
        for d in (2, 1, 3):
            start([rc(blocks, blocks, ("px", d, piece), xdev[d])])
        to_core(0, piece, first)

    for t in range(BITS):
        j = BITS - 1 - t
        size = 1 << t
        base_in = (s_own // size) * size
        theirs = base_in + (size - 2 * size * ((s_own // size) % 2))
        arrived(pan.at[x, c, pl.ds(theirs, size)] if t else pan.at[x, c, theirs], ("pz%d" % t))
        if t + 1 < BITS:
            nxt = 2 * size
            have = (s_own // nxt) * nxt
            start([rc(pan.at[x, c, pl.ds(have, nxt)], pan.at[x, c, pl.ds(have, nxt)],
                      "pz%d" % (t + 1), zdev[j - 1])])
        if t + 2 == BITS:
            over_x(0, have)

    over_x(1, theirs)

    @pl.when(root & (y == 1))
    def _():
        arrived(tt.at[0], "t0")

    @pl.when(root)
    def _():
        def tops(i, carry):
            for h in range(2):
                hi, mid, lo = split3(tt[h, pl.ds(i * 128, 128), :])
                at_row = pl.ds(h * ROWS + i * 128, 128)
                thm[at_row, 0:128] = hi
                thm[at_row, 128:256] = mid
                tlo[at_row, :] = lo
            return carry

        @pl.when(y == 0)
        def _():
            tt[1] = jnp.zeros((ROWS, COLS), F32)
        lax.fori_loop(0, ROWS // 128, tops, 0)
        slotc[...] = jnp.transpose(jnp.broadcast_to(slots[0:1, :], (128, NB)))

        def choose(i, carry):
            rows = pl.ds(i * 128, 128)
            lane = lax.broadcasted_iota(I32, (128, 128), 1)
            for b in range(SLOTS // 128):
                sel[rows, b * 128:(b + 1) * 128] = jnp.where(
                    (lane + b * 128).astype(F32) == slotc[rows, :], 1.0, 0.0).astype(BF16)
            return carry
        lax.fori_loop(0, 4 + 4 * y, choose, 0)

    @pl.when(root & (y == 1))
    def _():
        def pack(i, carry):
            ss = lax.broadcasted_iota(I32, (ZH * KC, NB), 0) + i * (ZH * KC)
            got = jnp.where(ss.astype(F32) == slots[0:1, :], 1.0, 0.0).astype(BF16)
            two = dot(got, thm[...])
            all3 = (two[:, :128] + two[:, 128:]) + dot(got, tlo[...])
            for z in range(ZH):
                dall[i, z] = all3[z * KC:(z + 1) * KC]
            return carry
        lax.fori_loop(0, Y, pack, 0)

    for d in range(1, Y):
        start([rc(dall.at[(y + d) % Y], dall.at[(y + d) % Y], "dy", ydev[d])], top & (y == 1))

    for z in (1, 3):
        @pl.when(top)
        def _():
            arrived(vall.at[y, z], "v%d" % z)
        to_roots(z)

    for d in (1, 3, 2):
        src = (x + X - d) % X
        arrived(pan.at[src, c, pl.ds(have, HALF)], ("px", d, 0))
        to_core(d, 0, have)

    @pl.when(top & (y != 1))
    def _():
        arrived(dall.at[y], "dy")
    start([rc(dall.at[y, 1], dme.at[pl.ds(0, KC)], "d", up),
           rc(dall.at[y, 3], dme.at[pl.ds(0, KC)], "d", down)], top)

    for d in (1, 3, 2):
        src = (x + X - d) % X
        arrived(pan.at[src, c, pl.ds(theirs, HALF)], ("px", d, 1))
        to_core(d, 1, theirs)

    @pl.when(top)
    def _():
        arrived(vall.at[y, 2], "v2")
    to_roots(2)
    start([rc(dall.at[y, 2], dfwd, "df", first)], top)

    for piece, mine_at in enumerate((have, theirs)):
        for d in range(X):
            arrived(pan.at[(x + X - d) % X, 1 - c, pl.ds(mine_at, HALF)], ("pc", d, piece))

    def psplit(i, carry):
        for cc in range(C):
            for s in range(ZL):
                hi, lo = split(pan[i, cc, s])
                rows = pl.ds((cc * ZL + s) * BLK, BLK)
                for q, line in enumerate(NATURAL):
                    phi[i, rows, line * QR:(line + 1) * QR] = hi[:, q * QR:(q + 1) * QR]
                    plo[i, rows, line * QR:(line + 1) * QR] = lo[:, q * QR:(q + 1) * QR]
        return carry
    lax.fori_loop(0, X, psplit, 0)

    @pl.when(root)
    def _():
        for d in range(1, Y):
            src = (y + Y - d) % Y
            for z in range(ZH):
                arrived(vall.at[src, z], ("vy", d, z))

        def vsplit(i, carry):
            for z in range(ZH):
                hi, lo = split(vall[i, z])
                vhl[pl.ds(i * (ZH * KC) + z * KC, KC), 0:128] = hi
                vhl[pl.ds(i * (ZH * KC) + z * KC, KC), 128:256] = lo
            return carry
        lax.fori_loop(0, Y, vsplit, 0)

        def form(i, q, line):
            rows = pl.ds(q * QR + i * 128, 128)
            sc = slotc[rows, :]
            moved = dot(sel[rows, :], vhl[...])
            stay = jnp.concatenate([sc, sc], axis=1) < 0.0
            phl[pl.ds(line * QR + i * 128, 128), :] = jnp.where(
                stay, thm[rows, :].astype(F32), moved).astype(BF16)

        def form_two(q, line):
            def body(i, carry):
                form(i, q, line)
                return carry
            lax.fori_loop(0, 2, body, 0)

        form_two(0, NATURAL[0])
        form_two(1, NATURAL[1])

        @pl.when(y == 0)
        def _():
            for line in NATURAL[2:]:
                phl[line * QR:(line + 1) * QR, :] = jnp.zeros((QR, 2 * COLS), BF16)

        @pl.when(y == 1)
        def _():
            form_two(2, NATURAL[2])
            form_two(3, NATURAL[3])

    def blocks(i, right, store, cols=slice(None)):
        two = dot(phi[i, :, cols], right[...])
        res = (two[:, :128] + two[:, 128:]) + dot(plo[i, :, cols], right[:, 0:128])
        for cc in range(C):
            for s in range(ZL):
                k = cc * ZL + s
                store(i * TILE + BLK * (rev(s) * C + cc), res[k * BLK:(k + 1) * BLK])

    def u_tile(i):
        h = i // 2
        line = y + h * (3 - 2 * y)

        @pl.when(root)
        def _():
            def store(row, val):
                ub[line, pl.ds(row - h * QR, BLK), :] = val
                out[pl.ds(row, BLK), :] = val
            blocks(i, phl, store)

    def chunk(line, k):
        return ub.at[line, pl.ds(k * CH, CH)]

    def ukey(rel, k):
        return ("u", rel, k)

    def send_chunk(line, rel, k, dev, cond):
        start([rc(chunk(line, k), chunk(line, k), ukey(rel, k), dev)], cond)

    firsts = [rc(chunk(y, k), chunk(y, k), ukey(0, k), first) for k in range(NCH)]

    def send_first(k, cond):
        @pl.when(cond)
        def _():
            firsts[k].start()

    r0, r1 = top & (y == 0), top & (y == 1)
    per = TILE // CH
    for i in (2, 3, 0, 1):
        u_tile(i)
        for k in range((i % 2) * per, (i % 2 + 1) * per):
            if i >= 2:
                send_chunk(3, 0, k, ydev[3], r0)
                send_chunk(2, 0, k, ydev[1], r1)
            else:
                send_first(k, root)
    for k in range(NCH):
        send_chunk(3, 1, k, ydev[2], r0)
        send_chunk(0, 2, k, ydev[2], r0)
        send_chunk(0, 1, k, ydev[3], r0)
        send_chunk(1, 3, k, ydev[1], r1)
        send_chunk(1, 2, k, ydev[2], r1)
        send_chunk(2, 3, k, ydev[2], r1)

    nonroot = top & (y >= 2)
    for k in range(NCH):
        @pl.when(nonroot)
        def _():
            arrived(chunk(y, k), ukey(0, k))
        send_first(k, nonroot)

    @pl.when(top)
    def _():
        for cp in firsts:
            cp.wait_send()

        @pl.when((zl > 0) & (zl < ZL - 1))
        def _():
            pl.semaphore_signal(token, inc=1, device_id=zdev[BITS - 1], device_id_type=MESH)

        @pl.when(zl == 1)
        def _():
            pl.semaphore_signal(token, inc=1, device_id=at(zl=ZL // 2), device_id_type=MESH)

        @pl.when(zl == ZL - 2)
        def _():
            pl.semaphore_signal(token, inc=1, device_id=at(zl=ZL // 2 - 1), device_id_type=MESH)
        pl.semaphore_wait(token, 1)
    for k in range(NCH):
        send_chunk(y, 0, k, second, top)

    @pl.when(via1 | via3)
    def _():
        arrived(dfwd, "df")
    start([rc(dfwd, dme.at[pl.ds(0, KC)], "d", up)], via1)
    start([rc(dfwd, dme.at[pl.ds(0, KC)], "d", down)], via3)

    @pl.when(nonroot)
    def _():
        dme[0:KC, :] = dall[y, 0]

    @pl.when(zh > 0)
    def _():
        arrived(dme.at[pl.ds(0, KC)], "d")

    @pl.when(notroot)
    def _():
        hit = jnp.sum(scat[...].astype(F32), axis=1, keepdims=True) > 0.0
        dh, dm, dl = split3(dme[...])
        moved = (dot(scat[...], dh) + dot(scat[...], dm)) + dot(scat[...], dl)
        base[...] = jnp.where(hit, moved, mat[...])

    for k in range(NCH):
        @pl.when(zh > 0)
        def _():
            arrived(chunk(y, k), ukey(0, k))
        send_chunk(y, 0, k, up, via1)
        send_chunk(y, 0, k, down, via3)
        for d in (2, 1, 3):
            send_chunk(y, Y - d, k, ydev[d], zh > 0)

    @pl.when(notroot)
    def _():
        def line_step(line, last):
            hi, lo = split(ub[line])
            uhl[:, 0:128] = hi
            uhl[:, 128:256] = lo
            at_col = pl.ds(pl.multiple_of(line * QR, QR), QR)

            def store(row, val):
                rows = pl.ds(row, BLK)
                if last:
                    out[rows, :] = base[rows, :] - val
                else:
                    base[rows, :] = base[rows, :] - val

            for i in range(X):
                blocks(i, uhl, store, at_col)

        line_step(y, False)
        for rel in (1, 3, 2):
            for k in range(NCH):
                arrived(chunk((y + rel) % Y, k), ukey(rel, k))
            line_step((y + rel) % Y, rel == 2)

    for cond, copies in pending:
        if cond is None:
            for cp in copies:
                cp.wait_send()
        else:
            @pl.when(cond)
            def _(copies=copies):
                for cp in copies:
                    cp.wait_send()


def per_device(matrix, panel, pivots):
    hbm, vmem = pl.BlockSpec(memory_space=pltpu.HBM), pl.BlockSpec(memory_space=pltpu.VMEM)
    return pl.pallas_call(
        kernel,
        out_shape=jax.ShapeDtypeStruct((ROWS, COLS), F32),
        in_specs=[hbm] * 3,
        out_specs=vmem,
        scratch_shapes=[
            pltpu.VMEM((ROWS, COLS), F32),
            pltpu.VMEM((1, NB), I32),
            pltpu.VMEM((X, C, ZL, BLK, NB), F32),
            pltpu.VMEM((X, TILE, NB), BF16),
            pltpu.VMEM((X, TILE, NB), BF16),
            pltpu.VMEM((KC, COLS), F32),
            pltpu.VMEM((Y, ZH, KC, COLS), F32),
            pltpu.VMEM((SLOTS, 2 * COLS), BF16),
            pltpu.VMEM((2, ROWS, COLS), F32),
            pltpu.VMEM((NB, 2 * COLS), BF16),
            pltpu.VMEM((NB, COLS), BF16),
            pltpu.VMEM((8, NB), F32),
            pltpu.VMEM((NB, 128), F32),
            pltpu.VMEM((NB, 2 * COLS), BF16),
            pltpu.VMEM((Y, ZH, KC, COLS), F32),
            pltpu.VMEM((128, COLS), F32),
            pltpu.VMEM((KC, COLS), F32),
            pltpu.VMEM((ROWS, 128), BF16),
            pltpu.VMEM((NB, SLOTS), BF16),
            pltpu.VMEM((ROWS, COLS), F32),
            pltpu.VMEM((4, ROWS // 2, COLS), F32),
            pltpu.VMEM((QR, 2 * COLS), BF16),
            pltpu.SemaphoreType.DMA((192,)),
            pltpu.SemaphoreType.DMA((64,)),
            pltpu.SemaphoreType.DMA((3,)),
            pltpu.SemaphoreType.REGULAR,
        ],
        compiler_params=pltpu.CompilerParams(
            collective_id=0, has_side_effects=True, vmem_limit_bytes=40 * 2**20
        ),
    )(matrix, panel, pivots.reshape(1, NB))


def solution(mesh):
    placed = (P("prow", "pcol"), P(("prow", "pcol"), None), P())
    return jax.shard_map(
        per_device, mesh=mesh, in_specs=placed, out_specs=P("prow", "pcol"), check_vma=False
    )
```

```python
import jax
import jax.numpy as jnp
from jax import lax
from jax.experimental import pallas as pl
from jax.experimental.pallas import tpu as pltpu
from jax.sharding import PartitionSpec as P

MESH = pl.DeviceIdType.MESH
F32, BF16, I32 = jnp.float32, jnp.bfloat16, jnp.int32

ZH, Y, X, ZL, C = 4, 4, 4, 8, 2
ROWS, NB, COLS = 512, 1024, 128
BLK = ROWS // (X * ZL * C)
KC = 48
SLOTS = ZH * Y * KC
CH, NCH = 64, 4
TILE = ROWS // X
NATURAL = (0, 3, 1, 2)
BITS = ZL.bit_length() - 1
HALF = ZL // 2
QR = NB // 4


def rev(s):
    return sum(((s >> j) & 1) << (BITS - 1 - j) for j in range(BITS))


def dot(a, b):
    return jnp.dot(a, b, preferred_element_type=F32)


def split(a):
    hi = a.astype(BF16)
    return hi, (a - hi.astype(F32)).astype(BF16)


def split3(a):
    hi = a.astype(BF16)
    rest = a - hi.astype(F32)
    mid = rest.astype(BF16)
    return hi, mid, (rest - mid.astype(F32)).astype(BF16)


def kernel(
    mat_hbm, pan_hbm, piv_hbm, out,
    mat, piv, pan, phi, plo, vloc, vall, vhl, tt, thm, tlo, slots, slotc, phl,
    dall, dme, dfwd, scat, sel, base, ub, uhl, send, recv, local, token,
):
    prow, pcol = lax.axis_index("prow"), lax.axis_index("pcol")
    zh, y = prow // Y, prow % Y
    x, zl, c = pcol // (ZL * C), (pcol // C) % ZL, pcol % C

    def at(zh=zh, y=y, x=x, zl=zl, c=c):
        return (zh * Y + y, x * (ZL * C) + zl * C + c)

    def bit(j):
        return (zl // (1 << j)) % 2

    ydev = [at(y=(y + d) % Y) for d in range(Y)]
    xdev = [at(x=(x + d) % X) for d in range(X)]
    zdev = [at(zl=zl + (1 << j) - (2 << j) * bit(j)) for j in range(BITS)]
    other = at(c=1 - c)
    up, down = at(zh=(zh + 1) % ZH), at(zh=(zh + ZH - 1) % ZH)
    near = ydev[1:] + xdev[1:] + zdev + [other]

    names = {}

    def num(key):
        return names.setdefault(key, len(names))

    counter = [0]

    def rc(src, dst, key, dev):
        sid = counter[0]
        counter[0] += 1
        return pltpu.make_async_remote_copy(
            src_ref=src, dst_ref=dst, send_sem=send.at[sid], recv_sem=recv.at[num(key)],
            device_id=dev, device_id_type=MESH,
        )

    def arrived(dst, key):
        pltpu.make_async_remote_copy(
            src_ref=dst, dst_ref=dst, send_sem=send.at[0], recv_sem=recv.at[num(key)],
            device_id=other, device_id_type=MESH,
        ).wait_recv()

    pending = []

    def start(copies, cond=None):
        pending.append((cond, copies))
        if cond is None:
            for cp in copies:
                cp.start()
        else:
            @pl.when(cond)
            def _():
                for cp in copies:
                    cp.start()

    top = zh == 0
    root = top & (y < 2)
    notroot = (zh > 0) | (y >= 2)
    inner = (zh == 1) | (zh == 3)
    low = zl // (ZL // 2)
    first = at(zh=3 - 2 * low)
    second = at(zh=1 + 2 * low)
    via1, via3 = (zh == 1) & (low == 1), (zh == 3) & (low == 0)

    barrier = pltpu.get_barrier_semaphore()

    @pl.when(top)
    def _():
        for z in (2, 1, 3):
            pl.semaphore_signal(barrier, inc=1, device_id=at(zh=z), device_id_type=MESH)
    for dev in near:
        pl.semaphore_signal(barrier, inc=1, device_id=dev, device_id_type=MESH)

    s_own = sum(bit(j) * (1 << (BITS - 1 - j)) for j in range(BITS))
    own = pan.at[x, c, s_own]
    loads = [pltpu.make_async_copy(piv_hbm, piv, local.at[0]),
             pltpu.make_async_copy(mat_hbm, mat, local.at[1]),
             pltpu.make_async_copy(pan_hbm, own, local.at[2])]
    for cp in loads:
        cp.start()
    loads[0].wait()

    def pack_own(prowv, slot):
        me = (y * ZH + zh) * KC
        kk = lax.broadcasted_iota(I32, (128, NB), 0)
        mine = (kk < KC) & ((kk + me).astype(F32) == slot)
        where_row = jnp.sum(
            jnp.where(mine, (prowv - prow * ROWS + 1).astype(F32), 0.0), axis=1, keepdims=True
        ) - 1.0
        pick = jnp.where(
            lax.broadcasted_iota(I32, (128, ROWS), 1).astype(F32) == where_row, 1.0, 0.0
        ).astype(F32)
        mh, mm, ml = split3(mat[...])
        pick16 = pick[:KC].astype(BF16)
        vloc[...] = (dot(pick16, mh) + dot(pick16, mm)) + dot(pick16, ml)
        scat[...] = jnp.transpose(pick).astype(BF16)

    prowv = piv[...]
    named = prowv >= NB
    group = (prowv // ROWS) % Y * ZH + (prowv // ROWS) // Y
    onehot = jnp.where(
        (lax.broadcasted_iota(I32, (ZH * Y, NB), 0) == group) & named, 1.0, 0.0
    ).astype(F32)
    tri = jnp.where(
        lax.broadcasted_iota(I32, (128, 128), 0) < lax.broadcasted_iota(I32, (128, 128), 1), 1.0, 0.0
    ).astype(BF16)
    before = jnp.zeros((ZH * Y, 1), F32)
    ranks = []
    for b in range(NB // 128):
        part = onehot[:, b * 128:(b + 1) * 128]
        count = dot(part.astype(BF16), tri) + before
        ranks.append(jnp.sum(count * part, axis=0, keepdims=True))
        before = before + jnp.sum(part, axis=1, keepdims=True)
    rank = jnp.concatenate(ranks, axis=1)
    slot = jnp.where(named, group.astype(F32) * KC + rank, -1.0)
    slots[...] = jnp.broadcast_to(slot, (8, NB))

    loads[1].wait()

    @pl.when(root)
    def _():
        vloc[...] = jnp.zeros((KC, COLS), F32)
        tt[y] = mat[...]

    @pl.when(notroot)
    def _():
        pack_own(prowv, slot)
    dme[KC:, :] = jnp.zeros((128 - KC, COLS), F32)

    @pl.when(top)
    def _():
        vall[y, 0] = vloc[...]

    loads[2].wait()
    pl.semaphore_wait(barrier, len(near) + (zh + ZH - 1) // ZH)

    j0 = BITS - 1
    start([rc(own, own, "pz0", zdev[j0])])
    start([rc(vloc, vall.at[y, 1], "v1", down)], zh == 1)
    start([rc(vloc, vall.at[y, 3], "v3", up)], zh == 3)
    start([rc(vloc, vall.at[y, 2], "v2", at(zh=(zh + 2) % ZH))], zh == 2)
    start([rc(mat, tt.at[0], "t0", ydev[1])], top & (y == 0))

    def to_roots(z):
        for d in range(1, Y):
            target = (y + d) % Y
            start([rc(vall.at[y, z], vall.at[y, z], ("vy", d, z), ydev[d])], top & (target < 2))

    to_roots(0)

    def to_core(d, piece, first):
        blocks = pan.at[(x + X - d) % X, c, pl.ds(first, HALF)]
        start([rc(blocks, blocks, ("pc", d, piece), other)])

    def over_x(piece, first):
        blocks = pan.at[x, c, pl.ds(first, HALF)]
        for d in (2, 1, 3):
            start([rc(blocks, blocks, ("px", d, piece), xdev[d])])
        to_core(0, piece, first)

    for t in range(BITS):
        j = BITS - 1 - t
        size = 1 << t
        base_in = (s_own // size) * size
        theirs = base_in + (size - 2 * size * ((s_own // size) % 2))
        arrived(pan.at[x, c, pl.ds(theirs, size)] if t else pan.at[x, c, theirs], ("pz%d" % t))
        if t + 1 < BITS:
            nxt = 2 * size
            have = (s_own // nxt) * nxt
            start([rc(pan.at[x, c, pl.ds(have, nxt)], pan.at[x, c, pl.ds(have, nxt)],
                      "pz%d" % (t + 1), zdev[j - 1])])
        if t + 2 == BITS:
            over_x(0, have)

    over_x(1, theirs)

    @pl.when(root & (y == 1))
    def _():
        arrived(tt.at[0], "t0")

    @pl.when(root)
    def _():
        def tops(i, carry):
            for h in range(2):
                hi, mid, lo = split3(tt[h, pl.ds(i * 128, 128), :])
                at_row = pl.ds(h * ROWS + i * 128, 128)
                thm[at_row, 0:128] = hi
                thm[at_row, 128:256] = mid
                tlo[at_row, :] = lo
            return carry

        @pl.when(y == 0)
        def _():
            tt[1] = jnp.zeros((ROWS, COLS), F32)
        lax.fori_loop(0, ROWS // 128, tops, 0)
        slotc[...] = jnp.transpose(jnp.broadcast_to(slots[0:1, :], (128, NB)))

        def choose(i, carry):
            rows = pl.ds(i * 128, 128)
            lane = lax.broadcasted_iota(I32, (128, 128), 1)
            for b in range(SLOTS // 128):
                sel[rows, b * 128:(b + 1) * 128] = jnp.where(
                    (lane + b * 128).astype(F32) == slotc[rows, :], 1.0, 0.0).astype(BF16)
            return carry
        lax.fori_loop(0, 4 + 4 * y, choose, 0)

    @pl.when(root & (y == 1))
    def _():
        def pack(i, carry):
            ss = lax.broadcasted_iota(I32, (ZH * KC, NB), 0) + i * (ZH * KC)
            got = jnp.where(ss.astype(F32) == slots[0:1, :], 1.0, 0.0).astype(BF16)
            two = dot(got, thm[...])
            all3 = (two[:, :128] + two[:, 128:]) + dot(got, tlo[...])
            for z in range(ZH):
                dall[i, z] = all3[z * KC:(z + 1) * KC]
            return carry
        lax.fori_loop(0, Y, pack, 0)

    for d in range(1, Y):
        start([rc(dall.at[(y + d) % Y], dall.at[(y + d) % Y], "dy", ydev[d])], top & (y == 1))

    for z in (1, 3):
        @pl.when(top)
        def _():
            arrived(vall.at[y, z], "v%d" % z)
        to_roots(z)

    for d in (1, 3, 2):
        src = (x + X - d) % X
        arrived(pan.at[src, c, pl.ds(have, HALF)], ("px", d, 0))
        to_core(d, 0, have)

    @pl.when(top & (y != 1))
    def _():
        arrived(dall.at[y], "dy")
    start([rc(dall.at[y, 1], dme.at[pl.ds(0, KC)], "d", up),
           rc(dall.at[y, 3], dme.at[pl.ds(0, KC)], "d", down)], top)

    for d in (1, 3, 2):
        src = (x + X - d) % X
        arrived(pan.at[src, c, pl.ds(theirs, HALF)], ("px", d, 1))
        to_core(d, 1, theirs)

    @pl.when(top)
    def _():
        arrived(vall.at[y, 2], "v2")
    to_roots(2)
    start([rc(dall.at[y, 2], dfwd, "df", first)], top)

    for piece, mine_at in enumerate((have, theirs)):
        for d in range(X):
            arrived(pan.at[(x + X - d) % X, 1 - c, pl.ds(mine_at, HALF)], ("pc", d, piece))

    def psplit(i, carry):
        for cc in range(C):
            for s in range(ZL):
                hi, lo = split(pan[i, cc, s])
                rows = pl.ds((cc * ZL + s) * BLK, BLK)
                for q, line in enumerate(NATURAL):
                    phi[i, rows, line * QR:(line + 1) * QR] = hi[:, q * QR:(q + 1) * QR]
                    plo[i, rows, line * QR:(line + 1) * QR] = lo[:, q * QR:(q + 1) * QR]
        return carry
    lax.fori_loop(0, X, psplit, 0)

    @pl.when(root)
    def _():
        for d in range(1, Y):
            src = (y + Y - d) % Y
            for z in range(ZH):
                arrived(vall.at[src, z], ("vy", d, z))

        def vsplit(i, carry):
            for z in range(ZH):
                hi, lo = split(vall[i, z])
                vhl[pl.ds(i * (ZH * KC) + z * KC, KC), 0:128] = hi
                vhl[pl.ds(i * (ZH * KC) + z * KC, KC), 128:256] = lo
            return carry
        lax.fori_loop(0, Y, vsplit, 0)

        def form(i, q, line):
            rows = pl.ds(q * QR + i * 128, 128)
            sc = slotc[rows, :]
            moved = dot(sel[rows, :], vhl[...])
            stay = jnp.concatenate([sc, sc], axis=1) < 0.0
            phl[pl.ds(line * QR + i * 128, 128), :] = jnp.where(
                stay, thm[rows, :].astype(F32), moved).astype(BF16)

        def form_two(q, line):
            def body(i, carry):
                form(i, q, line)
                return carry
            lax.fori_loop(0, 2, body, 0)

        form_two(0, NATURAL[0])
        form_two(1, NATURAL[1])

        @pl.when(y == 0)
        def _():
            for line in NATURAL[2:]:
                phl[line * QR:(line + 1) * QR, :] = jnp.zeros((QR, 2 * COLS), BF16)

        @pl.when(y == 1)
        def _():
            form_two(2, NATURAL[2])
            form_two(3, NATURAL[3])

    def blocks(i, right, store, cols=slice(None)):
        two = dot(phi[i, :, cols], right[...])
        res = (two[:, :128] + two[:, 128:]) + dot(plo[i, :, cols], right[:, 0:128])
        for cc in range(C):
            for s in range(ZL):
                k = cc * ZL + s
                store(i * TILE + BLK * (rev(s) * C + cc), res[k * BLK:(k + 1) * BLK])

    def u_tile(i):
        h = i // 2
        line = y + h * (3 - 2 * y)

        @pl.when(root)
        def _():
            def store(row, val):
                ub[line, pl.ds(row - h * QR, BLK), :] = val
                out[pl.ds(row, BLK), :] = val
            blocks(i, phl, store)

    def chunk(line, k):
        return ub.at[line, pl.ds(k * CH, CH)]

    def ukey(rel, k):
        return ("u", rel, k)

    def send_chunk(line, rel, k, dev, cond):
        start([rc(chunk(line, k), chunk(line, k), ukey(rel, k), dev)], cond)

    firsts = [rc(chunk(y, k), chunk(y, k), ukey(0, k), first) for k in range(NCH)]

    def send_first(k, cond):
        @pl.when(cond)
        def _():
            firsts[k].start()

    r0, r1 = top & (y == 0), top & (y == 1)
    per = TILE // CH
    for i in (2, 3, 0, 1):
        u_tile(i)
        for k in range((i % 2) * per, (i % 2 + 1) * per):
            if i >= 2:
                send_chunk(3, 0, k, ydev[3], r0)
                send_chunk(2, 0, k, ydev[1], r1)
            else:
                send_first(k, root)
    for k in range(NCH):
        send_chunk(3, 1, k, ydev[2], r0)
        send_chunk(0, 2, k, ydev[2], r0)
        send_chunk(0, 1, k, ydev[3], r0)
        send_chunk(1, 3, k, ydev[1], r1)
        send_chunk(1, 2, k, ydev[2], r1)
        send_chunk(2, 3, k, ydev[2], r1)

    nonroot = top & (y >= 2)
    for k in range(NCH):
        @pl.when(nonroot)
        def _():
            arrived(chunk(y, k), ukey(0, k))
        send_first(k, nonroot)

    inside = (zl > 0) & (zl < ZL - 1)

    @pl.when(top & inside)
    def _():
        for cp in firsts:
            cp.wait_send()
        pl.semaphore_signal(token, inc=1, device_id=zdev[BITS - 1], device_id_type=MESH)

        @pl.when(zl == 1)
        def _():
            pl.semaphore_signal(token, inc=1, device_id=at(zl=ZL // 2), device_id_type=MESH)

        @pl.when(zl == ZL - 2)
        def _():
            pl.semaphore_signal(token, inc=1, device_id=at(zl=ZL // 2 - 1), device_id_type=MESH)

    @pl.when(top)
    def _():
        pl.semaphore_wait(token, 1)
    for k in range(NCH):
        send_chunk(y, 0, k, second, top)
    pending.append((top & ((zl == 0) | (zl == ZL - 1)), firsts))

    @pl.when(via1 | via3)
    def _():
        arrived(dfwd, "df")
    start([rc(dfwd, dme.at[pl.ds(0, KC)], "d", up)], via1)
    start([rc(dfwd, dme.at[pl.ds(0, KC)], "d", down)], via3)

    @pl.when(nonroot)
    def _():
        dme[0:KC, :] = dall[y, 0]

    @pl.when(zh > 0)
    def _():
        arrived(dme.at[pl.ds(0, KC)], "d")

    @pl.when(notroot)
    def _():
        hit = jnp.sum(scat[...].astype(F32), axis=1, keepdims=True) > 0.0
        dh, dm, dl = split3(dme[...])
        moved = (dot(scat[...], dh) + dot(scat[...], dm)) + dot(scat[...], dl)
        base[...] = jnp.where(hit, moved, mat[...])

    for k in range(NCH):
        @pl.when(zh > 0)
        def _():
            arrived(chunk(y, k), ukey(0, k))
        send_chunk(y, 0, k, up, via1)
        send_chunk(y, 0, k, down, via3)
        for d in (2, 1, 3):
            send_chunk(y, Y - d, k, ydev[d], zh > 0)

    @pl.when(notroot)
    def _():
        def line_step(line, last):
            hi, lo = split(ub[line])
            uhl[:, 0:128] = hi
            uhl[:, 128:256] = lo
            at_col = pl.ds(pl.multiple_of(line * QR, QR), QR)

            def store(row, val):
                rows = pl.ds(row, BLK)
                if last:
                    out[rows, :] = base[rows, :] - val
                else:
                    base[rows, :] = base[rows, :] - val

            for i in range(X):
                blocks(i, uhl, store, at_col)

        line_step(y, False)
        for rel in (1, 3, 2):
            for k in range(NCH):
                arrived(chunk((y + rel) % Y, k), ukey(rel, k))
            line_step((y + rel) % Y, rel == 2)

    for cond, copies in pending:
        if cond is None:
            for cp in copies:
                cp.wait_send()
        else:
            @pl.when(cond)
            def _(copies=copies):
                for cp in copies:
                    cp.wait_send()


def per_device(matrix, panel, pivots):
    hbm, vmem = pl.BlockSpec(memory_space=pltpu.HBM), pl.BlockSpec(memory_space=pltpu.VMEM)
    return pl.pallas_call(
        kernel,
        out_shape=jax.ShapeDtypeStruct((ROWS, COLS), F32),
        in_specs=[hbm] * 3,
        out_specs=vmem,
        scratch_shapes=[
            pltpu.VMEM((ROWS, COLS), F32),
            pltpu.VMEM((1, NB), I32),
            pltpu.VMEM((X, C, ZL, BLK, NB), F32),
            pltpu.VMEM((X, TILE, NB), BF16),
            pltpu.VMEM((X, TILE, NB), BF16),
            pltpu.VMEM((KC, COLS), F32),
            pltpu.VMEM((Y, ZH, KC, COLS), F32),
            pltpu.VMEM((SLOTS, 2 * COLS), BF16),
            pltpu.VMEM((2, ROWS, COLS), F32),
            pltpu.VMEM((NB, 2 * COLS), BF16),
            pltpu.VMEM((NB, COLS), BF16),
            pltpu.VMEM((8, NB), F32),
            pltpu.VMEM((NB, 128), F32),
            pltpu.VMEM((NB, 2 * COLS), BF16),
            pltpu.VMEM((Y, ZH, KC, COLS), F32),
            pltpu.VMEM((128, COLS), F32),
            pltpu.VMEM((KC, COLS), F32),
            pltpu.VMEM((ROWS, 128), BF16),
            pltpu.VMEM((NB, SLOTS), BF16),
            pltpu.VMEM((ROWS, COLS), F32),
            pltpu.VMEM((4, ROWS // 2, COLS), F32),
            pltpu.VMEM((QR, 2 * COLS), BF16),
            pltpu.SemaphoreType.DMA((192,)),
            pltpu.SemaphoreType.DMA((64,)),
            pltpu.SemaphoreType.DMA((3,)),
            pltpu.SemaphoreType.REGULAR,
        ],
        compiler_params=pltpu.CompilerParams(
            collective_id=0, has_side_effects=True, vmem_limit_bytes=40 * 2**20
        ),
    )(matrix, panel, pivots.reshape(1, NB))


def solution(mesh):
    placed = (P("prow", "pcol"), P(("prow", "pcol"), None), P())
    return jax.shard_map(
        per_device, mesh=mesh, in_specs=placed, out_specs=P("prow", "pcol"), check_vma=False
    )
```

```python
import jax
import jax.numpy as jnp
from jax import lax
from jax.experimental import pallas as pl
from jax.experimental.pallas import tpu as pltpu
from jax.sharding import PartitionSpec as P

MESH = pl.DeviceIdType.MESH
F32, BF16, I32 = jnp.float32, jnp.bfloat16, jnp.int32

ZH, Y, X, ZL, C = 4, 4, 4, 8, 2
ROWS, NB, COLS = 512, 1024, 128
BLK = ROWS // (X * ZL * C)
KC = 48
SLOTS = ZH * Y * KC
CH, NCH = 64, 4
TILE = ROWS // X
NATURAL = (0, 3, 1, 2)
BITS = ZL.bit_length() - 1
HALF = ZL // 2
QR = NB // 4


def rev(s):
    return sum(((s >> j) & 1) << (BITS - 1 - j) for j in range(BITS))


def dot(a, b):
    return jnp.dot(a, b, preferred_element_type=F32)


def split(a):
    hi = a.astype(BF16)
    return hi, (a - hi.astype(F32)).astype(BF16)


def split3(a):
    hi = a.astype(BF16)
    rest = a - hi.astype(F32)
    mid = rest.astype(BF16)
    return hi, mid, (rest - mid.astype(F32)).astype(BF16)


def kernel(
    mat_hbm, pan_hbm, piv_hbm, out,
    mat, piv, pan, phi, plo, vloc, vall, vhl, tt, thm, tlo, slots, slotc, phl,
    dall, dme, dfwd, scat, sel, base, ub, uhl, send, recv, local, token,
):
    prow, pcol = lax.axis_index("prow"), lax.axis_index("pcol")
    zh, y = prow // Y, prow % Y
    x, zl, c = pcol // (ZL * C), (pcol // C) % ZL, pcol % C

    def at(zh=zh, y=y, x=x, zl=zl, c=c):
        return (zh * Y + y, x * (ZL * C) + zl * C + c)

    def bit(j):
        return (zl // (1 << j)) % 2

    ydev = [at(y=(y + d) % Y) for d in range(Y)]
    xdev = [at(x=(x + d) % X) for d in range(X)]
    zdev = [at(zl=zl + (1 << j) - (2 << j) * bit(j)) for j in range(BITS)]
    other = at(c=1 - c)
    up, down = at(zh=(zh + 1) % ZH), at(zh=(zh + ZH - 1) % ZH)
    near = ydev[1:] + xdev[1:] + zdev + [other]

    names = {}

    def num(key):
        return names.setdefault(key, len(names))

    counter = [0]

    def rc(src, dst, key, dev):
        sid = counter[0]
        counter[0] += 1
        return pltpu.make_async_remote_copy(
            src_ref=src, dst_ref=dst, send_sem=send.at[sid], recv_sem=recv.at[num(key)],
            device_id=dev, device_id_type=MESH,
        )

    def arrived(dst, key):
        pltpu.make_async_remote_copy(
            src_ref=dst, dst_ref=dst, send_sem=send.at[0], recv_sem=recv.at[num(key)],
            device_id=other, device_id_type=MESH,
        ).wait_recv()

    pending = []

    def start(copies, cond=None):
        pending.append((cond, copies))
        if cond is None:
            for cp in copies:
                cp.start()
        else:
            @pl.when(cond)
            def _():
                for cp in copies:
                    cp.start()

    top = zh == 0
    root = top & (y < 2)
    notroot = (zh > 0) | (y >= 2)
    inner = (zh == 1) | (zh == 3)
    low = zl // (ZL // 2)
    first = at(zh=3 - 2 * low)
    second = at(zh=1 + 2 * low)
    via1, via3 = (zh == 1) & (low == 1), (zh == 3) & (low == 0)

    barrier = pltpu.get_barrier_semaphore()

    @pl.when(top)
    def _():
        for z in (2, 1, 3):
            pl.semaphore_signal(barrier, inc=1, device_id=at(zh=z), device_id_type=MESH)
    for dev in near:
        pl.semaphore_signal(barrier, inc=1, device_id=dev, device_id_type=MESH)

    s_own = sum(bit(j) * (1 << (BITS - 1 - j)) for j in range(BITS))
    own = pan.at[x, c, s_own]
    loads = [pltpu.make_async_copy(piv_hbm, piv, local.at[0]),
             pltpu.make_async_copy(mat_hbm, mat, local.at[1]),
             pltpu.make_async_copy(pan_hbm, own, local.at[2])]
    for cp in loads:
        cp.start()
    loads[0].wait()

    def pack_own(prowv, slot):
        me = (y * ZH + zh) * KC
        kk = lax.broadcasted_iota(I32, (128, NB), 0)
        mine = (kk < KC) & ((kk + me).astype(F32) == slot)
        where_row = jnp.sum(
            jnp.where(mine, (prowv - prow * ROWS + 1).astype(F32), 0.0), axis=1, keepdims=True
        ) - 1.0
        pick = jnp.where(
            lax.broadcasted_iota(I32, (128, ROWS), 1).astype(F32) == where_row, 1.0, 0.0
        ).astype(F32)
        mh, mm, ml = split3(mat[...])
        pick16 = pick[:KC].astype(BF16)
        vloc[...] = (dot(pick16, mh) + dot(pick16, mm)) + dot(pick16, ml)
        scat[...] = jnp.transpose(pick).astype(BF16)

    prowv = piv[...]
    named = prowv >= NB
    group = (prowv // ROWS) % Y * ZH + (prowv // ROWS) // Y
    onehot = jnp.where(
        (lax.broadcasted_iota(I32, (ZH * Y, NB), 0) == group) & named, 1.0, 0.0
    ).astype(F32)
    tri = jnp.where(
        lax.broadcasted_iota(I32, (128, 128), 0) < lax.broadcasted_iota(I32, (128, 128), 1), 1.0, 0.0
    ).astype(BF16)
    before = jnp.zeros((ZH * Y, 1), F32)
    ranks = []
    for b in range(NB // 128):
        part = onehot[:, b * 128:(b + 1) * 128]
        count = dot(part.astype(BF16), tri) + before
        ranks.append(jnp.sum(count * part, axis=0, keepdims=True))
        before = before + jnp.sum(part, axis=1, keepdims=True)
    rank = jnp.concatenate(ranks, axis=1)
    slot = jnp.where(named, group.astype(F32) * KC + rank, -1.0)
    slots[...] = jnp.broadcast_to(slot, (8, NB))

    loads[1].wait()

    @pl.when(root)
    def _():
        vloc[...] = jnp.zeros((KC, COLS), F32)
        tt[y] = mat[...]

    @pl.when(notroot)
    def _():
        pack_own(prowv, slot)
    dme[KC:, :] = jnp.zeros((128 - KC, COLS), F32)

    @pl.when(top)
    def _():
        vall[y, 0] = vloc[...]

    loads[2].wait()
    pl.semaphore_wait(barrier, len(near) + (zh + ZH - 1) // ZH)

    j0 = BITS - 1
    start([rc(own, own, "pz0", zdev[j0])])
    start([rc(vloc, vall.at[y, 1], "v1", down)], zh == 1)
    start([rc(vloc, vall.at[y, 3], "v3", up)], zh == 3)
    start([rc(vloc, vall.at[y, 2], "v2", at(zh=(zh + 2) % ZH))], zh == 2)
    start([rc(mat, tt.at[0], "t0", ydev[1])], top & (y == 0))

    def to_roots(z):
        for d in range(1, Y):
            target = (y + d) % Y
            start([rc(vall.at[y, z], vall.at[y, z], ("vy", d, z), ydev[d])], top & (target < 2))

    to_roots(0)

    def to_core(d, piece, first):
        blocks = pan.at[(x + X - d) % X, c, pl.ds(first, HALF)]
        start([rc(blocks, blocks, ("pc", d, piece), other)])

    def over_x(piece, first):
        blocks = pan.at[x, c, pl.ds(first, HALF)]
        for d in (2, 1, 3):
            start([rc(blocks, blocks, ("px", d, piece), xdev[d])])
        to_core(0, piece, first)

    for t in range(BITS):
        j = BITS - 1 - t
        size = 1 << t
        base_in = (s_own // size) * size
        theirs = base_in + (size - 2 * size * ((s_own // size) % 2))
        arrived(pan.at[x, c, pl.ds(theirs, size)] if t else pan.at[x, c, theirs], ("pz%d" % t))
        if t + 1 < BITS:
            nxt = 2 * size
            have = (s_own // nxt) * nxt
            start([rc(pan.at[x, c, pl.ds(have, nxt)], pan.at[x, c, pl.ds(have, nxt)],
                      "pz%d" % (t + 1), zdev[j - 1])])
        if t + 2 == BITS:
            over_x(0, have)

    over_x(1, theirs)

    @pl.when(root & (y == 1))
    def _():
        arrived(tt.at[0], "t0")

    @pl.when(root)
    def _():
        def tops(i, carry):
            for h in range(2):
                hi, mid, lo = split3(tt[h, pl.ds(i * 128, 128), :])
                at_row = pl.ds(h * ROWS + i * 128, 128)
                thm[at_row, 0:128] = hi
                thm[at_row, 128:256] = mid
                tlo[at_row, :] = lo
            return carry

        @pl.when(y == 0)
        def _():
            tt[1] = jnp.zeros((ROWS, COLS), F32)
        lax.fori_loop(0, ROWS // 128, tops, 0)
        slotc[...] = jnp.transpose(jnp.broadcast_to(slots[0:1, :], (128, NB)))

        def choose(i, carry):
            rows = pl.ds(i * 128, 128)
            lane = lax.broadcasted_iota(I32, (128, 128), 1)
            for b in range(SLOTS // 128):
                sel[rows, b * 128:(b + 1) * 128] = jnp.where(
                    (lane + b * 128).astype(F32) == slotc[rows, :], 1.0, 0.0).astype(BF16)
            return carry
        lax.fori_loop(0, 4 + 4 * y, choose, 0)

    @pl.when(root & (y == 1))
    def _():
        def pack(i, carry):
            ss = lax.broadcasted_iota(I32, (ZH * KC, NB), 0) + i * (ZH * KC)
            got = jnp.where(ss.astype(F32) == slots[0:1, :], 1.0, 0.0).astype(BF16)
            two = dot(got, thm[...])
            all3 = (two[:, :128] + two[:, 128:]) + dot(got, tlo[...])
            for z in range(ZH):
                dall[i, z] = all3[z * KC:(z + 1) * KC]
            return carry
        lax.fori_loop(0, Y, pack, 0)

    for d in range(1, Y):
        start([rc(dall.at[(y + d) % Y], dall.at[(y + d) % Y], "dy", ydev[d])], top & (y == 1))

    for z in (1, 3):
        @pl.when(top)
        def _():
            arrived(vall.at[y, z], "v%d" % z)
        to_roots(z)

    for d in (1, 3, 2):
        src = (x + X - d) % X
        arrived(pan.at[src, c, pl.ds(have, HALF)], ("px", d, 0))
        to_core(d, 0, have)

    @pl.when(top & (y != 1))
    def _():
        arrived(dall.at[y], "dy")
    start([rc(dall.at[y, 1], dme.at[pl.ds(0, KC)], "d", up),
           rc(dall.at[y, 3], dme.at[pl.ds(0, KC)], "d", down)], top)

    for d in (1, 3, 2):
        src = (x + X - d) % X
        arrived(pan.at[src, c, pl.ds(theirs, HALF)], ("px", d, 1))
        to_core(d, 1, theirs)

    @pl.when(top)
    def _():
        arrived(vall.at[y, 2], "v2")
    to_roots(2)
    start([rc(dall.at[y, 2], dfwd, "df", first)], top)

    for piece, mine_at in enumerate((have, theirs)):
        for d in range(X):
            arrived(pan.at[(x + X - d) % X, 1 - c, pl.ds(mine_at, HALF)], ("pc", d, piece))

    def psplit(i, carry):
        for cc in range(C):
            for s in range(ZL):
                hi, lo = split(pan[i, cc, s])
                rows = pl.ds((cc * ZL + s) * BLK, BLK)
                for q, line in enumerate(NATURAL):
                    phi[i, rows, line * QR:(line + 1) * QR] = hi[:, q * QR:(q + 1) * QR]
                    plo[i, rows, line * QR:(line + 1) * QR] = lo[:, q * QR:(q + 1) * QR]
        return carry
    lax.fori_loop(0, X, psplit, 0)

    @pl.when(root)
    def _():
        for d in range(1, Y):
            src = (y + Y - d) % Y
            for z in range(ZH):
                arrived(vall.at[src, z], ("vy", d, z))

        for i in range(Y):
            for z in range(ZH):
                hi, lo = split(vall[i, z])
                vhl[pl.ds(i * (ZH * KC) + z * KC, KC), 0:128] = hi
                vhl[pl.ds(i * (ZH * KC) + z * KC, KC), 128:256] = lo

        def form(i, q, line):
            rows = pl.ds(q * QR + i * 128, 128)
            sc = slotc[rows, :]
            moved = dot(sel[rows, :], vhl[...])
            stay = jnp.concatenate([sc, sc], axis=1) < 0.0
            phl[pl.ds(line * QR + i * 128, 128), :] = jnp.where(
                stay, thm[rows, :].astype(F32), moved).astype(BF16)

        def form_two(q, line):
            for i in range(QR // 128):
                form(i, q, line)

        form_two(0, NATURAL[0])
        form_two(1, NATURAL[1])

        @pl.when(y == 0)
        def _():
            for line in NATURAL[2:]:
                phl[line * QR:(line + 1) * QR, :] = jnp.zeros((QR, 2 * COLS), BF16)

        @pl.when(y == 1)
        def _():
            form_two(2, NATURAL[2])
            form_two(3, NATURAL[3])

    def blocks(i, right, store, cols=slice(None)):
        two = dot(phi[i, :, cols], right[...])
        res = (two[:, :128] + two[:, 128:]) + dot(plo[i, :, cols], right[:, 0:128])
        for cc in range(C):
            for s in range(ZL):
                k = cc * ZL + s
                store(i * TILE + BLK * (rev(s) * C + cc), res[k * BLK:(k + 1) * BLK])

    def u_tile(i):
        h = i // 2
        line = y + h * (3 - 2 * y)

        @pl.when(root)
        def _():
            def store(row, val):
                ub[line, pl.ds(row - h * QR, BLK), :] = val
                out[pl.ds(row, BLK), :] = val
            blocks(i, phl, store)

    def chunk(line, k):
        return ub.at[line, pl.ds(k * CH, CH)]

    def ukey(rel, k):
        return ("u", rel, k)

    def send_chunk(line, rel, k, dev, cond):
        start([rc(chunk(line, k), chunk(line, k), ukey(rel, k), dev)], cond)

    firsts = [rc(chunk(y, k), chunk(y, k), ukey(0, k), first) for k in range(NCH)]

    def send_first(k, cond):
        @pl.when(cond)
        def _():
            firsts[k].start()

    r0, r1 = top & (y == 0), top & (y == 1)
    per = TILE // CH
    for i in (2, 3, 0, 1):
        u_tile(i)
        for k in range((i % 2) * per, (i % 2 + 1) * per):
            if i >= 2:
                send_chunk(3, 0, k, ydev[3], r0)
                send_chunk(2, 0, k, ydev[1], r1)
            else:
                send_first(k, root)
    for k in range(NCH):
        send_chunk(3, 1, k, ydev[2], r0)
        send_chunk(0, 2, k, ydev[2], r0)
        send_chunk(0, 1, k, ydev[3], r0)
        send_chunk(1, 3, k, ydev[1], r1)
        send_chunk(1, 2, k, ydev[2], r1)
        send_chunk(2, 3, k, ydev[2], r1)

    nonroot = top & (y >= 2)
    for k in range(NCH):
        @pl.when(nonroot)
        def _():
            arrived(chunk(y, k), ukey(0, k))
        send_first(k, nonroot)

    inside = (zl > 0) & (zl < ZL - 1)

    @pl.when(top & inside)
    def _():
        for cp in firsts:
            cp.wait_send()
        pl.semaphore_signal(token, inc=1, device_id=zdev[BITS - 1], device_id_type=MESH)

        @pl.when(zl == 1)
        def _():
            pl.semaphore_signal(token, inc=1, device_id=at(zl=ZL // 2), device_id_type=MESH)

        @pl.when(zl == ZL - 2)
        def _():
            pl.semaphore_signal(token, inc=1, device_id=at(zl=ZL // 2 - 1), device_id_type=MESH)

    @pl.when(top)
    def _():
        pl.semaphore_wait(token, 1)
    for k in range(NCH):
        send_chunk(y, 0, k, second, top)
    pending.append((top & ((zl == 0) | (zl == ZL - 1)), firsts))

    @pl.when(via1 | via3)
    def _():
        arrived(dfwd, "df")
    start([rc(dfwd, dme.at[pl.ds(0, KC)], "d", up)], via1)
    start([rc(dfwd, dme.at[pl.ds(0, KC)], "d", down)], via3)

    @pl.when(nonroot)
    def _():
        dme[0:KC, :] = dall[y, 0]

    @pl.when(zh > 0)
    def _():
        arrived(dme.at[pl.ds(0, KC)], "d")

    @pl.when(notroot)
    def _():
        hit = jnp.sum(scat[...].astype(F32), axis=1, keepdims=True) > 0.0
        dh, dm, dl = split3(dme[...])
        moved = (dot(scat[...], dh) + dot(scat[...], dm)) + dot(scat[...], dl)
        base[...] = jnp.where(hit, moved, mat[...])

    for k in range(NCH):
        @pl.when(zh > 0)
        def _():
            arrived(chunk(y, k), ukey(0, k))
        send_chunk(y, 0, k, up, via1)
        send_chunk(y, 0, k, down, via3)
        for d in (2, 1, 3):
            send_chunk(y, Y - d, k, ydev[d], zh > 0)

    @pl.when(notroot)
    def _():
        def line_step(line, last):
            hi, lo = split(ub[line])
            uhl[:, 0:128] = hi
            uhl[:, 128:256] = lo
            at_col = pl.ds(pl.multiple_of(line * QR, QR), QR)

            def store(row, val):
                rows = pl.ds(row, BLK)
                if last:
                    out[rows, :] = base[rows, :] - val
                else:
                    base[rows, :] = base[rows, :] - val

            for i in range(X):
                blocks(i, uhl, store, at_col)

        line_step(y, False)
        for rel in (1, 3, 2):
            for k in range(NCH):
                arrived(chunk((y + rel) % Y, k), ukey(rel, k))
            line_step((y + rel) % Y, rel == 2)

    for cond, copies in pending:
        if cond is None:
            for cp in copies:
                cp.wait_send()
        else:
            @pl.when(cond)
            def _(copies=copies):
                for cp in copies:
                    cp.wait_send()


def per_device(matrix, panel, pivots):
    hbm, vmem = pl.BlockSpec(memory_space=pltpu.HBM), pl.BlockSpec(memory_space=pltpu.VMEM)
    return pl.pallas_call(
        kernel,
        out_shape=jax.ShapeDtypeStruct((ROWS, COLS), F32),
        in_specs=[hbm] * 3,
        out_specs=vmem,
        scratch_shapes=[
            pltpu.VMEM((ROWS, COLS), F32),
            pltpu.VMEM((1, NB), I32),
            pltpu.VMEM((X, C, ZL, BLK, NB), F32),
            pltpu.VMEM((X, TILE, NB), BF16),
            pltpu.VMEM((X, TILE, NB), BF16),
            pltpu.VMEM((KC, COLS), F32),
            pltpu.VMEM((Y, ZH, KC, COLS), F32),
            pltpu.VMEM((SLOTS, 2 * COLS), BF16),
            pltpu.VMEM((2, ROWS, COLS), F32),
            pltpu.VMEM((NB, 2 * COLS), BF16),
            pltpu.VMEM((NB, COLS), BF16),
            pltpu.VMEM((8, NB), F32),
            pltpu.VMEM((NB, 128), F32),
            pltpu.VMEM((NB, 2 * COLS), BF16),
            pltpu.VMEM((Y, ZH, KC, COLS), F32),
            pltpu.VMEM((128, COLS), F32),
            pltpu.VMEM((KC, COLS), F32),
            pltpu.VMEM((ROWS, 128), BF16),
            pltpu.VMEM((NB, SLOTS), BF16),
            pltpu.VMEM((ROWS, COLS), F32),
            pltpu.VMEM((4, ROWS // 2, COLS), F32),
            pltpu.VMEM((QR, 2 * COLS), BF16),
            pltpu.SemaphoreType.DMA((192,)),
            pltpu.SemaphoreType.DMA((64,)),
            pltpu.SemaphoreType.DMA((3,)),
            pltpu.SemaphoreType.REGULAR,
        ],
        compiler_params=pltpu.CompilerParams(
            collective_id=0, has_side_effects=True, vmem_limit_bytes=40 * 2**20
        ),
    )(matrix, panel, pivots.reshape(1, NB))


def solution(mesh):
    placed = (P("prow", "pcol"), P(("prow", "pcol"), None), P())
    return jax.shard_map(
        per_device, mesh=mesh, in_specs=placed, out_specs=P("prow", "pcol"), check_vma=False
    )
```
